32 devices in a mesh: gx: 4 (over y, x), gy: 8 (over z, core).
Axes of the slice: x: 2, y: 2, z: 4, core: 2. Of those that a mesh axis runs over, the one named last changes fastest.
Arguments:
- rhs: bfloat16 [256, 384, 128], P(('gx', 'gy')), may hold values from -6 to 6
- diag_blocks: bfloat16 [256, 384, 384], P(('gx', 'gy'))
- inverse_blocks: bfloat16 [256, 384, 384], P(('gx', 'gy'))
- couplings: bfloat16 [256, 6, 384, 96], P(('gx', 'gy')), may hold values from -0.25 to 0.25
- prolong: bfloat16 [384, 48], replicated, may hold values from -0.3125 to 0.3125
- face_source: int32 [256, 6], P(('gx', 'gy')), may hold values from 0 to 5, as said below
- subset: int32 [256], P(('gx', 'gy')), may hold values from 0 to 7
Outputs:
- solution: float32 [256, 384, 128], P(('gx', 'gy'))
The draws below stay inside these ranges and needn't reach their ends.
Inputs may be any that keep to these rules, and one draw needn't show every extreme that they name: `face_source`: face f of an element and face f xor 1 of its neighbour are both boundary faces or both not. A face that is not a boundary face has code 1 where its neighbour lies inside the same partition and the code of its direction otherwise; face 4 at k = 0 and face 5 at k = 1 are boundary faces. `subset`: subsets of different rows of partitions are different.
All inputs are finite; a program needn't handle non-finite values.
Results may differ from the reference program's by a relative error of at most 0.0055.
Values may be sent and summed in bfloat16 or wider, within the bound.
No kernel may reach another device: no remote copies, remote signals or barrier semaphores. Data moves between devices by JAX's collectives and lax.ppermute only.
A program may use at most 64 MiB of HBM per device.

```python
import math
import jax
import jax.numpy as jnp
import numpy as np
from jax import lax

NVAR = 6
NP = 4
NRHS = 128
EZ = 2
CITER = 4
E_DEV = 8
DOF = 384
FDOF = 96
CDOF = 48
ELEMS = 256
SUBS = 8
N_GX = 4
N_GY = 8


def draw_block_set(key):
    noise = jax.random.normal(key, (ELEMS, DOF, DOF), jnp.float32)
    blocks = jnp.eye(DOF, dtype=jnp.float32)[None] + noise * (0.3 / math.sqrt(DOF))
    return blocks.astype(jnp.bfloat16)


def draw_diag_blocks(key, part):
    return draw_block_set(jax.random.fold_in(key, 11))


def draw_inverse_blocks(key, part):
    return draw_block_set(jax.random.fold_in(key, 23))


def draw_face_source(key, part):
    cells_x = 2 * N_GX
    cells_y = 2 * N_GY
    open_x = jax.random.randint(jax.random.fold_in(key, 5), (cells_x, cells_y, EZ), 0, 8) > 0
    open_y = jax.random.randint(jax.random.fold_in(key, 7), (cells_x, cells_y, EZ), 0, 8) > 0
    element = jnp.arange(ELEMS, dtype=jnp.int32)
    device = element // E_DEV
    local = element % E_DEV
    row_pos = device // N_GY
    col_pos = device % N_GY
    place_i = local % 2
    place_j = local // 2 % 2
    place_k = local // 4
    cell_x = row_pos * 2 + place_i
    cell_y = col_pos * 2 + place_j
    live0 = open_x[(cell_x - 1) % cells_x, cell_y, place_k]
    live1 = open_x[cell_x, cell_y, place_k]
    live2 = open_y[cell_x, (cell_y - 1) % cells_y, place_k]
    live3 = open_y[cell_x, cell_y, place_k]
    live4 = place_k > 0
    live5 = place_k < EZ - 1
    code0 = jnp.where(place_i == 1, 1, 2)
    code1 = jnp.where(place_i == 0, 1, 3)
    code2 = jnp.where(place_j == 1, 1, 4)
    code3 = jnp.where(place_j == 0, 1, 5)
    ones = jnp.ones_like(local)
    lives = [live0, live1, live2, live3, live4, live5]
    codes = [code0, code1, code2, code3, ones, ones]
    columns = [jnp.where(lives[index], codes[index], 0) for index in range(6)]
    return jnp.stack(columns, axis=1).astype(jnp.int32)


def touch_ends(drawn, key, low, top_value):
    dims = drawn.shape
    spot = [jax.random.randint(jax.random.fold_in(key, axis), (), 0, dims[axis]) for axis in range(len(dims))]
    drawn = drawn.at[tuple(spot)].set(low)
    longest = dims.index(max(dims))
    spot[longest] = (spot[longest] + 1) % dims[longest]
    return drawn.at[tuple(spot)].set(top_value)


def block_levels(key, dims, pieces, low, top_value):
    factor_of = 1.0
    for position, parts in pieces:
        steps = jax.random.uniform(jax.random.fold_in(jax.random.fold_in(key, 6), position), (parts,), jnp.float32, low / len(pieces), top_value / len(pieces))
        factor_of = factor_of * jnp.repeat(jnp.exp(steps), dims[position] // parts).reshape((-1,) + (1,) * (len(dims) - 1 - position))
    return factor_of


def rank_bounds(number_of, lean):
    loads = [(1 << 20) // math.isqrt(standing ** lean) + 1 for standing in range(1, number_of + 1)]
    spread = 1 + sum(loads) // (1 << 30)
    return np.cumsum(np.array([max(1, weight // spread) for weight in loads]))


def ranked_ids(own_key, shape, number_of, skew):
    grid = rank_bounds(number_of, skew)
    ticket = jax.random.randint(jax.random.fold_in(own_key, 1), shape, 0, int(grid[number_of - 1]))
    rank = jnp.searchsorted(jnp.asarray(grid, jnp.int32), ticket, side="right")
    return jax.random.permutation(jax.random.fold_in(own_key, 2), number_of)[rank].astype(jnp.int32)


def scatter_about(own_key, shape, scale, reach, cuts=(), held_as=jnp.bfloat16):
    loudness = block_levels(own_key, shape, cuts, -0.22, 0.18) if cuts else 1.0
    values = jax.random.normal(own_key, shape, jnp.float32) * scale * loudness
    return jnp.minimum(jnp.maximum(values, -reach), reach).astype(held_as)


def setup_inputs(seed: int = 0) -> dict:
    seeds = jax.random.split(jax.random.key(seed), 8)
    return {
        "rhs": scatter_about(seeds[0], (ELEMS, DOF, NRHS), 1.0, 6.0, ((0, 32),)),
        "diag_blocks": draw_diag_blocks(jax.random.fold_in(seeds[7], 71), 0),
        "inverse_blocks": draw_inverse_blocks(jax.random.fold_in(seeds[7], 71), 0),
        "couplings": scatter_about(seeds[3], (ELEMS, 6, DOF, FDOF), (6 * FDOF) ** -0.5, 0.25, ((0, 32),)),
        "prolong": scatter_about(seeds[4], (DOF, CDOF), DOF ** -0.5, 0.3125),
        "face_source": draw_face_source(jax.random.fold_in(seeds[7], 71), 0),
        "subset": touch_ends(ranked_ids(seeds[6], (ELEMS,), SUBS, 2), jax.random.fold_in(seeds[6], 3), 0, SUBS - 1).astype(jnp.int32),
    }


def face_trace(values, face_id):
    leading = values.shape[0]
    columns = values.shape[-1]
    volume = values.reshape(leading, NVAR, NP, NP, NP, columns)
    sliced = lax.index_in_dim(volume, (NP - 1) * (face_id % 2), 4 - face_id // 2, keepdims=False)
    return sliced.reshape(leading, NVAR * NP * NP, columns)


def blockwise(function, arrays):
    blocks = ELEMS // E_DEV
    split = tuple(array_item.reshape((blocks, E_DEV) + array_item.shape[1:]) for array_item in arrays)
    result = lax.map(lambda items: function(*items), split)
    return result.reshape((ELEMS,) + result.shape[2:])


def neighbour_ids(face_source):
    element = jnp.arange(ELEMS, dtype=jnp.int32)
    device = element // E_DEV
    local = element % E_DEV
    row_pos = device // N_GY
    col_pos = device % N_GY
    row_shift = jnp.array([0, 0, -1, 1, 0, 0], dtype=jnp.int32)
    col_shift = jnp.array([0, 0, 0, 0, -1, 1], dtype=jnp.int32)
    flips = jnp.array([1, 1, 2, 2, 0, 0], dtype=jnp.int32)
    layer_step = jnp.array([0, 0, 0, 0, -4, 4], dtype=jnp.int32)
    near_local = jnp.clip(jnp.bitwise_xor(local[:, None], flips[None, :]) + layer_step[None, :], 0, E_DEV - 1)
    target_row = (row_pos[:, None] + row_shift[face_source]) % N_GX
    target_col = (col_pos[:, None] + col_shift[face_source]) % N_GY
    return ((target_row * N_GY + target_col) * E_DEV + near_local).astype(jnp.int32)


def batch_diag(blocks, state_b):
    return jnp.einsum("edk,ekr->edr", blocks.astype(jnp.float32), state_b.astype(jnp.float32))


def batch_faces(couplings, near):
    return jnp.einsum("efdt,eftr->edr", couplings.astype(jnp.float32), near.astype(jnp.float32))


def residual_of(state, rhs, diag_blocks, couplings, neighbours, live):
    state_b = state.astype(jnp.bfloat16)
    traces = jnp.stack([face_trace(state_b, face_id) for face_id in range(6)], axis=1)
    near = jnp.stack([traces[:, face_id ^ 1][neighbours[:, face_id]] for face_id in range(6)], axis=1)
    near = jnp.where(live[:, :, None, None], near, jnp.zeros_like(near))
    local_part = blockwise(batch_diag, (diag_blocks, state_b))
    remote_part = blockwise(batch_faces, (couplings, near))
    return rhs.astype(jnp.float32) - local_part - remote_part


def reference(rhs, diag_blocks, inverse_blocks, couplings, prolong, face_source, subset):
    neighbours = neighbour_ids(face_source)
    live = face_source > 0
    first = 0.7 * blockwise(batch_diag, (inverse_blocks, rhs))
    resid = residual_of(first, rhs, diag_blocks, couplings, neighbours, live)
    resid_b = resid.astype(jnp.bfloat16)
    prolong_f = prolong.astype(jnp.float32)
    restricted = jnp.einsum("dc,edr->ecr", prolong_f, resid_b.astype(jnp.float32))
    face_rows = jnp.stack([face_trace(prolong[None], face_id ^ 1)[0] for face_id in range(6)], axis=0)
    masked_rows = jnp.where(live[:, :, None, None], face_rows[None], jnp.zeros_like(face_rows[None]))

    def stiff_block(blocks, coupled, rows):
        inner = jnp.einsum("edk,kc->edc", blocks.astype(jnp.float32), prolong_f)
        outer = jnp.einsum("efdt,eftc->edc", coupled.astype(jnp.float32), rows.astype(jnp.float32))
        return inner + outer

    stiff = blockwise(stiff_block, (diag_blocks, couplings, masked_rows)).astype(jnp.bfloat16)
    block = jnp.einsum("dc,edk->eck", prolong_f, stiff.astype(jnp.float32))
    element = jnp.arange(ELEMS, dtype=jnp.int32)
    group_key = ((element // E_DEV) // N_GY * SUBS + subset).astype(jnp.int32)
    groups = N_GX * SUBS
    coarse_rhs = jax.ops.segment_sum(restricted, group_key, groups)
    coarse_matrix = jax.ops.segment_sum(block, group_key, groups)
    members = jax.ops.segment_sum(jnp.ones((ELEMS,), jnp.float32), group_key, groups)
    theta = 0.5 / jnp.maximum(members, 1.0)
    coarse = jnp.zeros_like(coarse_rhs)
    for sweep in range(CITER):
        applied = jnp.einsum("sck,skr->scr", coarse_matrix, coarse, precision=lax.Precision.HIGHEST)
        coarse = coarse + theta[:, None, None] * (coarse_rhs - applied)
    coarse_b = coarse.astype(jnp.bfloat16)
    picked = coarse_b[group_key]
    state = first + jnp.einsum("dc,ecr->edr", prolong_f, picked.astype(jnp.float32))
    for sweep in range(2):
        resid = residual_of(state, rhs, diag_blocks, couplings, neighbours, live)
        state = state + 0.7 * blockwise(batch_diag, (inverse_blocks, resid.astype(jnp.bfloat16)))
    return state
```

```python
import functools

import jax
import jax.numpy as jnp
from jax import lax
from jax.experimental import pallas as pl
from jax.experimental.pallas import tpu as pltpu
from jax.sharding import PartitionSpec as P

NVAR = 6
NP = 4
CITER = 4

relax_fine = 0.7
relax_coarse = 0.5

F32 = jnp.float32
BF16 = jnp.bfloat16
LIMIT = 40 * 1024 * 1024


def dot(a, b, precision=None):
    return jnp.dot(a, b, preferred_element_type=F32, precision=precision)


def place(e):
    return lax.rem(e, 2), lax.rem(lax.div(e, 2), 2), lax.div(e, 4)


def whole(shape):
    return pl.BlockSpec(shape, lambda e: (0,) * len(shape))


def each(shape):
    return pl.BlockSpec((1,) + shape, lambda e: (e,) + (0,) * len(shape))


def scalars():
    return pl.BlockSpec(memory_space=pltpu.SMEM)


def run(body, ins, in_specs, outs, out_specs, scratch, grid, flops):
    size = sum(a.size * a.dtype.itemsize for a in list(ins) + list(outs))
    return pl.pallas_call(
        body,
        grid=grid,
        in_specs=in_specs,
        out_specs=out_specs,
        out_shape=outs,
        scratch_shapes=scratch,
        compiler_params=pltpu.CompilerParams(vmem_limit_bytes=LIMIT),
        cost_estimate=pl.CostEstimate(flops=flops, bytes_accessed=size, transcendentals=0),
    )(*ins)


def read_traces(load, tmp):
    side = NP * NP
    layers = NVAR * NP
    faces = [load(0, layers * NP, NP), load(NP - 1, layers * NP, NP)]
    for g in (0, 1):
        for ii in range(NP):
            tmp[g, pl.ds(ii, layers, stride=NP), :] = load(g * NP * (NP - 1) + ii, layers, side)
        faces.append(tmp[g])
    for g in (0, 1):
        faces.append(
            jnp.concatenate(
                [load((v * NP + g * (NP - 1)) * side, side, 1) for v in range(NVAR)], axis=0
            )
        )
    return faces


def emit_traces(e, state_ref, tr_ref, gxm, gxp, gym, gyp, tmp):
    def load(start, size, stride):
        if stride == 1:
            return state_ref[0, pl.ds(start, size), :]
        return state_ref[0, pl.ds(start, size, stride=stride), :]

    faces = [face.astype(BF16) for face in read_traces(load, tmp)]
    for f in range(6):
        tr_ref[0, f] = faces[f]
    i, j, k = place(e)
    at_x = lax.div(e, 2)
    at_y = i + 2 * k

    @pl.when(i == 0)
    def _():
        gxm[at_x] = faces[0]

    @pl.when(i == 1)
    def _():
        gxp[at_x] = faces[1]

    @pl.when(j == 0)
    def _():
        gym[at_y] = faces[2]

    @pl.when(j == 1)
    def _():
        gyp[at_y] = faces[3]


def masked(face_source, e, f, value):
    return jnp.where(face_source[e, f] > 0, value, jnp.zeros_like(value))


def first_body(rhs, inv, first, tr, gxm, gxp, gym, gyp, tmp):
    e = pl.program_id(0)
    first[0] = relax_fine * dot(inv[0], rhs[0])
    emit_traces(e, first, tr, gxm, gxp, gym, gyp, tmp)


def local_body(rhs, state, diag, coup, tr, prolong, face_source, subset, acc, mats, pf, pt, wide, tmp, msum):
    e = pl.program_id(0)
    last = pl.num_programs(0) - 1
    coarse = prolong.shape[1]

    @pl.when(e == 0)
    def _():
        wide[...] = jnp.zeros_like(wide)
        wide[:, 0:coarse] = prolong[...].astype(F32)

        def load(start, size, stride):
            if stride == 1:
                return wide[pl.ds(start, size), :]
            return wide[pl.ds(start, size, stride=stride), :]

        for f, face in enumerate(read_traces(load, tmp)):
            pf[f] = face.astype(BF16)
        pt[...] = wide[...].T[0:coarse].astype(BF16)
        msum[...] = jnp.zeros_like(msum)

    i, j, k = place(e)
    cols = acc.shape[2]
    both = jnp.concatenate([state[0].astype(BF16), wide[...].astype(BF16)], axis=1)
    total = dot(diag[0], both)
    for f, near, face in (
        (1 - i, jnp.bitwise_xor(e, 1), i),
        (3 - j, jnp.bitwise_xor(e, 2), 2 + j),
        (5 - k, jnp.bitwise_xor(e, 4), 4 + k),
    ):
        rows = jnp.concatenate([tr[near, face], pf[face]], axis=1)
        total = total + dot(coup[0, f], masked(face_source, e, f, rows))
    acc[0] = rhs[0].astype(F32) - total[:, 0:cols]
    stiff = total[:, cols:]
    for f, face in ((i, 1 - i), (2 + j, 3 - j)):
        stiff = stiff + dot(coup[0, f], masked(face_source, e, f, pf[face]))
    block = dot(pt[...], stiff.astype(BF16))
    lane = lax.broadcasted_iota(jnp.int32, block.shape, 1)
    s = subset[e]
    msum[s] += block + jnp.where(lane == coarse, 1.0, 0.0)
    msum[0] += jnp.where(lane == coarse + 1 + e, s.astype(F32), 0.0)

    @pl.when(e == last)
    def _():
        mats[...] = msum[...].astype(BF16)


def pick_x(e, from_m, from_p):
    i = lax.rem(e, 2)
    at = lax.div(e, 2)
    return jnp.where(i == 0, from_m[at], from_p[at])


def pick_y(e, from_m, from_p):
    i, j, k = place(e)
    at = i + 2 * k
    return jnp.where(j == 0, from_m[at], from_p[at])


def restrict_body(part, cx, cy, xm, xp, ym, yp, pt, face_source, subset, resid, sums, total):
    e = pl.program_id(0)
    i, j, k = place(e)

    @pl.when(e == 0)
    def _():
        total[...] = jnp.zeros_like(total)

    r = part[0] - dot(cx[0, 0], masked(face_source, e, i, pick_x(e, xm, xp)))
    r = r - dot(cy[0, 0], masked(face_source, e, 2 + j, pick_y(e, ym, yp)))
    resid[0] = r
    total[subset[e]] += dot(pt[...], r.astype(BF16))

    @pl.when(e == pl.num_programs(0) - 1)
    def _():
        sums[...] = total[...].astype(BF16)


def coarse_body(one, two, mats, subset, y_all, y_m, y_p):
    groups = one.shape[0]
    coarse = one.shape[1]
    high = lax.Precision.HIGHEST
    rights, blocks, thetas, ys = [], [], [], []
    for s in range(groups):
        block = mats[0, s].astype(F32)
        for d in range(1, mats.shape[0]):
            block = block + mats[d, s].astype(F32)
        theta = relax_coarse / jnp.maximum(block[:, coarse : coarse + 1], 1.0)
        right = one[s].astype(F32) + two[s].astype(F32)
        rights.append(right)
        blocks.append(block[:, 0:coarse])
        thetas.append(theta)
        ys.append(theta * right)
    for sweep in range(CITER - 1):
        applied = [dot(blocks[s], ys[s], high) for s in range(groups)]
        ys = [ys[s] + thetas[s] * (rights[s] - applied[s]) for s in range(groups)]
    for s in range(groups):
        y_all[s] = ys[s].astype(BF16)
    for e in range(subset.shape[0]):
        (y_p if e % 2 else y_m)[e // 2] = y_all[subset[e]]


def second_body(resid, state, diag, coup, y_all, prolong, pf, face_source, subset, near_sets, acc, second):
    e = pl.program_id(0)
    i, j, k = place(e)
    coarse = prolong.shape[1]
    step = dot(prolong[...], y_all[subset[e]])
    second[0] = state[0] + step
    total = dot(diag[0], step.astype(BF16))
    for f, s, face in (
        (1 - i, subset[jnp.bitwise_xor(e, 1)], i),
        (3 - j, subset[jnp.bitwise_xor(e, 2)], 2 + j),
        (5 - k, subset[jnp.bitwise_xor(e, 4)], 4 + k),
        (2 + j, near_sets[j, jnp.bitwise_xor(e, 2)], 3 - j),
    ):
        rows = dot(pf[face][:, 0:coarse], y_all[s]).astype(BF16)
        total = total + dot(coup[0, f], masked(face_source, e, f, rows))
    acc[0] = resid[0] - total


def smooth_body(part, second, cx, inv, ym, yp, pf, face_source, state, tr, gxm, gxp, gym, gyp, tmp):
    e = pl.program_id(0)
    i, j, k = place(e)
    coarse = ym.shape[1]
    rows = dot(pf[1 - i][:, 0:coarse], pick_x(e, ym, yp)).astype(BF16)
    r = part[0] - dot(cx[0, 0], masked(face_source, e, i, rows))
    state[0] = second[0] + relax_fine * dot(inv[0], r.astype(BF16))
    emit_traces(e, state, tr, gxm, gxp, gym, gyp, tmp)


def inner_body(rhs, state, diag, coup, tr, face_source, acc):
    e = pl.program_id(0)
    i, j, k = place(e)
    total = dot(diag[0], state[0].astype(BF16))
    for f, near, face in (
        (1 - i, jnp.bitwise_xor(e, 1), i),
        (3 - j, jnp.bitwise_xor(e, 2), 2 + j),
        (5 - k, jnp.bitwise_xor(e, 4), 4 + k),
    ):
        total = total + dot(coup[0, f], masked(face_source, e, f, tr[near, face]))
    acc[0] = rhs[0].astype(F32) - total


def final_body(part, state, cx, cy, inv, xm, xp, ym, yp, face_source, out):
    e = pl.program_id(0)
    i, j, k = place(e)
    r = part[0] - dot(cx[0, 0], masked(face_source, e, i, pick_x(e, xm, xp)))
    r = r - dot(cy[0, 0], masked(face_source, e, 2 + j, pick_y(e, ym, yp)))
    out[0] = state[0] + relax_fine * dot(inv[0], r.astype(BF16))


def shift(value, axis, step):
    count = lax.axis_size(axis)
    return lax.ppermute(value, axis, [(i, (i + step) % count) for i in range(count)])


def exchange(sends):
    gxm, gxp, gym, gyp = sends
    return (
        shift(gxp, "gx", 1),
        shift(gxm, "gx", -1),
        shift(gyp, "gy", 1),
        shift(gym, "gy", -1),
    )


def row_sum(part):
    count = lax.axis_size("gy")
    if count & (count - 1):
        return lax.psum(part, "gy"), jnp.zeros_like(part)
    step = 1
    while True:
        other = lax.ppermute(part, "gy", [(i, i ^ step) for i in range(count)])
        step *= 2
        if step >= count:
            return part, other
        part = (part.astype(F32) + other.astype(F32)).astype(BF16)


def on_device(rhs, diag_blocks, inverse_blocks, couplings, prolong, face_source, subset):
    elements, dof, cols = rhs.shape
    fdof = couplings.shape[3]
    coarse = prolong.shape[1]
    groups = lax.axis_size("gy")
    grid = (elements,)
    half = elements // 2
    shape = jax.ShapeDtypeStruct
    state_s = shape((elements, dof, cols), F32)
    tr_s = shape((elements, 6, fdof, cols), BF16)
    send_s = shape((half, fdof, cols), BF16)
    sends_s = [send_s] * 4
    fine = each((dof, cols))
    square = each((dof, dof))
    faces = each((6, dof, fdof))
    traced = each((6, fdof, cols))
    side = whole((half, fdof, cols))
    face_x = pl.BlockSpec((1, 1, dof, fdof), lambda e: (e, lax.rem(e, 2), 0, 0))
    face_y = pl.BlockSpec((1, 1, dof, fdof), lambda e: (e, 2 + lax.rem(lax.div(e, 2), 2), 0, 0))
    tmp = pltpu.VMEM((2, fdof, cols), F32)
    apply_flops = 2 * elements * dof * cols * (dof + 3 * fdof)
    inv_flops = 2 * elements * dof * dof * cols
    far_flops = 4 * elements * dof * fdof * cols

    first, tr, *sends = run(
        first_body,
        (rhs, inverse_blocks),
        [fine, square],
        [state_s, tr_s] + sends_s,
        [fine, traced] + [side] * 4,
        [tmp],
        grid,
        inv_flops,
    )
    xm, xp, ym, yp = exchange(sends)
    acc, mats, pf, pt = run(
        local_body,
        (rhs, first, diag_blocks, couplings, tr, prolong, face_source, subset),
        [fine, fine, square, faces, whole(tr.shape), whole(prolong.shape), scalars(), scalars()],
        [
            state_s,
            shape((groups, coarse, cols), BF16),
            shape((6, fdof, cols), BF16),
            shape((coarse, dof), BF16),
        ],
        [
            fine,
            whole((groups, coarse, cols)),
            whole((6, fdof, cols)),
            whole((coarse, dof)),
        ],
        [pltpu.VMEM((dof, cols), F32), tmp, pltpu.VMEM((groups, coarse, cols), F32)],
        grid,
        2 * apply_flops,
    )
    all_mats = lax.all_gather(mats, "gy", axis=0)
    all_sets = all_mats[:, 0, 0, coarse + 1 : coarse + 1 + elements].astype(jnp.int32)
    me = lax.axis_index("gy")
    near_sets = jnp.stack(
        [
            lax.dynamic_index_in_dim(all_sets, (me - 1) % groups, 0, keepdims=False),
            lax.dynamic_index_in_dim(all_sets, (me + 1) % groups, 0, keepdims=False),
        ]
    )
    resid, sums = run(
        restrict_body,
        (acc, couplings, couplings, xm, xp, ym, yp, pt, face_source, subset),
        [fine, face_x, face_y, side, side, side, side, whole(pt.shape), scalars(), scalars()],
        [state_s, shape((groups, coarse, cols), BF16)],
        [fine, whole((groups, coarse, cols))],
        [pltpu.VMEM((groups, coarse, cols), F32)],
        grid,
        far_flops,
    )
    one, two = row_sum(sums)
    y_s = shape((half, coarse, cols), BF16)
    vmem = pl.BlockSpec(memory_space=pltpu.VMEM)
    y_all, y_m, y_p = run(
        coarse_body,
        (one, two, all_mats, subset),
        [vmem, vmem, vmem, scalars()],
        [shape((groups, coarse, cols), BF16), y_s, y_s],
        [vmem, vmem, vmem],
        [],
        (),
        6 * 2 * groups * coarse * coarse * cols * CITER,
    )
    yxm = shift(y_p, "gx", 1)
    yxp = shift(y_m, "gx", -1)
    acc, second = run(
        second_body,
        (resid, first, diag_blocks, couplings, y_all, prolong, pf, face_source, subset, near_sets),
        [
            fine,
            fine,
            square,
            faces,
            whole(y_all.shape),
            whole(prolong.shape),
            whole(pf.shape),
            scalars(),
            scalars(),
            scalars(),
        ],
        [state_s, state_s],
        [fine, fine],
        [],
        grid,
        apply_flops,
    )
    state, tr, *sends = run(
        smooth_body,
        (acc, second, couplings, inverse_blocks, yxm, yxp, pf, face_source),
        [fine, fine, face_x, square, whole(y_m.shape), whole(y_m.shape), whole(pf.shape), scalars()],
        [state_s, tr_s] + sends_s,
        [fine, traced] + [side] * 4,
        [tmp],
        grid,
        inv_flops,
    )
    xm, xp, ym, yp = exchange(sends)
    acc = run(
        inner_body,
        (rhs, state, diag_blocks, couplings, tr, face_source),
        [fine, fine, square, faces, whole(tr.shape), scalars()],
        [state_s],
        [fine],
        [],
        grid,
        apply_flops,
    )[0]
    return run(
        final_body,
        (acc, state, couplings, couplings, inverse_blocks, xm, xp, ym, yp, face_source),
        [fine, fine, face_x, face_y, square, side, side, side, side, scalars()],
        [state_s],
        [fine],
        [],
        grid,
        inv_flops + far_flops,
    )[0]


def solution(mesh):
    return jax.shard_map(
        on_device,
        mesh=mesh,
        in_specs=(
            P(("gx", "gy"), None, None),
            P(("gx", "gy"), None, None),
            P(("gx", "gy"), None, None),
            P(("gx", "gy"), None, None, None),
            P(),
            P(("gx", "gy"), None),
            P(("gx", "gy")),
        ),
        out_specs=P(("gx", "gy"), None, None),
        check_vma=False,
    )
```

```python
import jax
import jax.numpy as jnp
from jax import lax
from jax.experimental import pallas as pl
from jax.experimental.pallas import tpu as pltpu
from jax.sharding import PartitionSpec as P

NVAR = 6
NP = 4
CITER = 4

relax_fine = 0.7
relax_coarse = 0.5

F32 = jnp.float32
BF16 = jnp.bfloat16
LIMIT = 24 * 1024 * 1024


def dot(a, b, precision=None):
    return jnp.dot(a, b, preferred_element_type=F32, precision=precision)


def place(e):
    return e % 2, e // 2 % 2, e // 4


def run(body, ins, outs, scratch, flops, far_ins=(), far_outs=()):
    size = sum(a.size * a.dtype.itemsize for a in list(ins) + list(outs))
    vmem = pl.BlockSpec(memory_space=pltpu.VMEM)
    smem = pl.BlockSpec(memory_space=pltpu.SMEM)
    hbm = pl.BlockSpec(memory_space=pltpu.HBM)
    ins = [
        pltpu.with_memory_space_constraint(a, pltpu.HBM) if n in far_ins else a
        for n, a in enumerate(ins)
    ]
    return pl.pallas_call(
        body,
        in_specs=[
            smem if a.dtype == jnp.int32 else hbm if n in far_ins else vmem
            for n, a in enumerate(ins)
        ],
        out_specs=[hbm if n in far_outs else vmem for n in range(len(outs))],
        out_shape=list(outs),
        scratch_shapes=scratch,
        compiler_params=pltpu.CompilerParams(vmem_limit_bytes=LIMIT),
        cost_estimate=pl.CostEstimate(flops=flops, bytes_accessed=size, transcendentals=0),
    )(*ins)


def fetch(e, pairs, sems):
    return [pltpu.make_async_copy(a.at[e], b.at[e], sems.at[n, e]) for n, (a, b) in enumerate(pairs)]


def begin(count, pairs, sems):
    for e in range(count):
        for copy in fetch(e, pairs, sems):
            copy.start()


def finish(e, pairs, sems):
    for copy in fetch(e, pairs, sems):
        copy.wait()


def read_traces(load, tmp):
    side = NP * NP
    layers = NVAR * NP
    faces = [load(0, layers * NP, NP), load(NP - 1, layers * NP, NP)]
    for g in (0, 1):
        for ii in range(NP):
            tmp[g, pl.ds(ii, layers, stride=NP), :] = load(g * NP * (NP - 1) + ii, layers, side)
        faces.append(tmp[g])
    for g in (0, 1):
        faces.append(
            jnp.concatenate(
                [load((v * NP + g * (NP - 1)) * side, side, 1) for v in range(NVAR)], axis=0
            )
        )
    return faces


def strided(ref):
    def load(start, size, stride):
        if stride == 1:
            return ref[pl.ds(start, size), :]
        return ref[pl.ds(start, size, stride=stride), :]

    return load


def emit_traces(e, state_ref, tr_ref, sides, tmp):
    faces = [f.astype(BF16) for f in read_traces(strided(state_ref.at[e]), tmp.at[e])]
    i, j, k = place(e)
    for f in (1 - i, 3 - j, 5 - k):
        tr_ref[e, f] = faces[f]
    sides[i, e // 2] = faces[i]
    sides[2 + j, i + 2 * k] = faces[2 + j]


def order(spots):
    return lax.rem(spots[3], 2) == 0, lax.rem(spots[0], 2) == 0


def pack_sends(spots, low, high, near, far):
    near[...] = jnp.where(spots, high, low)
    far[...] = jnp.where(spots, low, high)


def emit_sends(spots, sides, sends):
    for axis, even in enumerate(order(spots)):
        pack_sends(even, sides[2 * axis], sides[2 * axis + 1], sends[2 * axis], sends[2 * axis + 1])


def masked(face_source, e, f, value):
    return jnp.where(face_source[e, f] > 0, value, jnp.zeros_like(value))


def inner_faces(e):
    i, j, k = place(e)
    return (1 - i, e ^ 1, i), (3 - j, e ^ 2, 2 + j), (5 - k, e ^ 4, 4 + k)


def stack(parts, rows):
    have = sum(part.shape[0] for part in parts)
    if have < rows:
        parts = parts + [jnp.zeros((rows - have, parts[0].shape[1]), parts[0].dtype)]
    return jnp.concatenate(parts, axis=0)


def came(even, from_near, from_far, upper, at):
    first, second = (from_near, from_far) if upper else (from_far, from_near)
    return jnp.where(even, first[at], second[at])


def pick(e, halo, face_source, spots):
    i, j, k = place(e)
    even_x, even_y = order(spots)
    return [
        masked(face_source, e, i, came(even_x, halo[0], halo[1], i, e // 2)),
        masked(face_source, e, 2 + j, came(even_y, halo[2], halo[3], j, i + 2 * k)),
    ]


def first_body(rhs_far, inv_far, spots, first, tr, rhs, inv, s0, s1, s2, s3, tmp, sides, sems):
    pairs = ((inv_far, inv), (rhs_far, rhs))
    count = rhs.shape[0]
    begin(count, pairs, sems)
    for e in range(count):
        finish(e, pairs, sems)
        first[e] = relax_fine * dot(inv[e], rhs[e])
        emit_traces(e, first, tr, sides, tmp)
    emit_sends(spots, sides, (s0, s1, s2, s3))


def local_body(
    rhs, state, diag_far, coup_far, tr, pt, face_source, subset,
    acc, mats, oper, outer, pf, prolong,
    diag, coup, wide, tmp, msum, sems,
):
    coarse, dof = pt.shape
    count, _, cols = acc.shape
    near_rows = outer.shape[2]
    pairs = ((diag_far, diag), (coup_far, coup))
    begin(count, pairs, sems)
    wide[...] = stack([pt[...].astype(F32)], cols).T
    for f, face in enumerate(read_traces(strided(wide), tmp)):
        pf[f] = face.astype(BF16)
    base = wide[...].astype(BF16)
    prolong[...] = base
    msum[...] = jnp.zeros_like(msum)
    for e in range(count):
        i, j, k = place(e)
        inner = inner_faces(e)
        finish(e, pairs, sems)
        oper[e, :, 0:dof] = diag[e]
        oper[e, :, dof : 2 * dof] = stack([coup[e, f] for f, near, face in inner], dof).T
        outer[e] = stack([coup[e, i], coup[e, 2 + j]], near_rows).T
    stiffs = []
    for e in range(count):
        i, j, k = place(e)
        inner = inner_faces(e)
        values = [state[e].astype(BF16)] + [
            masked(face_source, e, f, tr[near, face]) for f, near, face in inner
        ]
        bases = [base] + [masked(face_source, e, f, pf[face]) for f, near, face in inner]
        both = jnp.concatenate([stack(values, 2 * dof), stack(bases, 2 * dof)], axis=1)
        total = dot(oper[e], both)
        acc[e] = rhs[e].astype(F32) - total[:, 0:cols]
        far = stack(
            [masked(face_source, e, i, pf[1 - i]), masked(face_source, e, 2 + j, pf[3 - j])],
            near_rows,
        )
        stiffs.append((total[:, cols:] + dot(outer[e], far)).astype(BF16))
    blocks = [dot(pt[...], stiff) for stiff in stiffs]
    lane = lax.broadcasted_iota(jnp.int32, (coarse, cols), 1)
    one = jnp.where(lane == coarse, 1.0, 0.0)
    for e in range(count):
        msum[subset[e]] += blocks[e] + one
    for s in range(mats.shape[0]):
        block = msum[s]
        low = jnp.where(lane == coarse, 0.0, block)[coarse // 2 :]
        mats[s] = block[: coarse // 2] + pltpu.roll(low, cols // 2, 1)


def restrict_body(part, outer, xm, xp, ym, yp, pt, mats, face_source, subset, spots, resid, keep, give, total):
    count = part.shape[0]
    coarse = pt.shape[0]
    total[...] = jnp.zeros_like(total)
    for e in range(count):
        far = stack(pick(e, (xm, xp, ym, yp), face_source, spots), outer.shape[2])
        resid[e] = part[e] - dot(outer[e], far)
    shares = [dot(pt[...], resid[e].astype(BF16)) for e in range(count)]
    for e in range(count):
        total[subset[e]] += shares[e]
    row = lax.broadcasted_iota(jnp.int32, (count, mats.shape[2]), 0)
    lane = lax.broadcasted_iota(jnp.int32, row.shape, 1)
    half = lax.rem(spots[0], 2)
    mine = (lane >= row.shape[1] // 2) == (half == 1)
    names = jnp.zeros(row.shape, F32)
    for e in range(count):
        names = jnp.where(mine & (row == e), subset[e].astype(F32), names)
    share = keep.shape[0]
    for which, ref in ((half, keep), (1 - half, give)):
        for s in range(share):
            own = jnp.where(lax.div(spots[0], 2) == s, names, 0.0)
            ref[s, 0:coarse] = total[which * share + s].astype(BF16)
            rest = stack([mats[which * share + s], own], ref.shape[1] - coarse)
            ref[s, coarse:] = rest.astype(BF16)


def split(value):
    high = value.astype(BF16)
    return high, (value - high.astype(F32)).astype(BF16)


def coarse_body(one, two, spots, y_own, names):
    groups, coarse, cols = y_own.shape
    half = coarse // 2
    rights, blocks, thetas, ys = [], [], [], []
    for s in range(groups):
        both = one[s].astype(F32) + two[s].astype(F32)
        right = both[0:coarse]
        packed = both[coarse : coarse + half]
        block = jnp.concatenate([packed, pltpu.roll(packed, cols // 2, 1)], axis=0)
        theta = relax_coarse / jnp.maximum(packed[:, coarse : coarse + 1], 1.0)
        theta = jnp.concatenate([theta, theta], axis=0)
        high, low = split(block[:, 0:coarse])
        rights.append(right)
        blocks.append(jnp.concatenate([high, high, low], axis=1))
        thetas.append(theta)
        ys.append(theta * right)
    for sweep in range(CITER - 1):
        sides = []
        for s in range(groups):
            high, low = split(ys[s])
            sides.append(jnp.concatenate([high, low, high], axis=0))
        applied = [dot(blocks[s], sides[s]) for s in range(groups)]
        ys = [ys[s] + thetas[s] * (rights[s] - applied[s]) for s in range(groups)]
    for s in range(groups):
        y_own[s] = ys[s].astype(BF16)
    start = coarse + half
    count = names.shape[1]
    lane = lax.broadcasted_iota(jnp.int32, (count, cols), 1)
    for side in (0, 1):
        slot = lax.div(spots[1 + side], 2)
        far = one[slot].astype(F32) + two[slot].astype(F32)
        mine = (lane >= cols // 2) == (lax.rem(spots[1 + side], 2) == 1)
        far = jnp.where(mine, far[start : start + count], 0.0)
        names[side] = far + pltpu.roll(far, cols // 2, 1)


def choose_body(y_own, y_other, subset, spots, y_all, near, far, sides):
    share = y_own.shape[0]
    half = lax.rem(spots[0], 2)
    for s in range(share):
        y_all[half * share + s] = y_own[s]
        y_all[(1 - half) * share + s] = y_other[s]
    for e in range(subset.shape[0]):
        sides[e % 2, e // 2] = y_all[subset[e]]
    pack_sends(order(spots)[0], sides[0], sides[1], near, far)


def second_body(resid, state, oper, outer, y_all, prolong, pf, names, face_source, subset, acc, second):
    coarse = y_all.shape[1]
    count, dof, _ = resid.shape
    inside, outside = [], []
    for e in range(count):
        i, j, k = place(e)
        step = dot(prolong[:, 0:coarse], y_all[subset[e]])
        second[e] = state[e] + step
        values = [step.astype(BF16)]
        for f, near, face in inner_faces(e):
            rows = dot(pf[face, :, 0:coarse], y_all[subset[near]]).astype(BF16)
            values.append(masked(face_source, e, f, rows))
        name = names[j, pl.ds(e ^ 2, 1), :]
        y_far = jnp.zeros(y_all.shape[1:], F32)
        for s in range(y_all.shape[0]):
            y_far = jnp.where(name == float(s), y_all[s].astype(F32), y_far)
        rows = dot(pf[3 - j, :, 0:coarse], y_far.astype(BF16)).astype(BF16)
        far = [jnp.zeros_like(rows), masked(face_source, e, 2 + j, rows)]
        inside.append(stack(values, 2 * dof))
        outside.append(stack(far, outer.shape[2]))
    for e in range(count):
        acc[e] = resid[e] - (dot(oper[e], inside[e]) + dot(outer[e], outside[e]))


def smooth_body(part, second, outer, inv, y0, y1, pf, face_source, spots, state, tr, s0, s1, s2, s3, tmp, sides, res):
    coarse = y0.shape[1]
    count = part.shape[0]
    rows = []
    for e in range(count):
        i = e % 2
        y_far = came(order(spots)[0], y0, y1, i, e // 2)
        value = dot(pf[1 - i, :, 0:coarse], y_far).astype(BF16)
        rows.append(stack([masked(face_source, e, i, value)], outer.shape[2]))
    for e in range(count):
        res[e] = (part[e] - dot(outer[e], rows[e])).astype(BF16)
    for e in range(count):
        state[e] = second[e] + relax_fine * dot(inv[e], res[e])
        emit_traces(e, state, tr, sides, tmp)
    emit_sends(spots, sides, (s0, s1, s2, s3))


def inner_body(rhs, state, oper, tr, face_source, acc):
    dof = state.shape[1]
    for e in range(state.shape[0]):
        values = [state[e].astype(BF16)] + [
            masked(face_source, e, f, tr[near, face]) for f, near, face in inner_faces(e)
        ]
        acc[e] = rhs[e].astype(F32) - dot(oper[e], stack(values, 2 * dof))


def final_body(part, state, outer, inv, xm, xp, ym, yp, face_source, spots, out_far, res, out, sems):
    count = state.shape[0]
    pairs = ((out, out_far),)
    for e in range(count):
        far = stack(pick(e, (xm, xp, ym, yp), face_source, spots), outer.shape[2])
        res[e] = (part[e] - dot(outer[e], far)).astype(BF16)
    for e in range(count):
        out[e] = state[e] + relax_fine * dot(inv[e], res[e])
        fetch(e, pairs, sems)[0].start()
    for e in range(count):
        finish(e, pairs, sems)


def swap(value, axis, start):
    count = lax.axis_size(axis)
    pairs = [(i % count, (i + 1) % count) for i in range(start, count, 2)]
    return lax.ppermute(value, axis, pairs + [(b, a) for a, b in pairs])


def exchange(sends):
    x0, x1, y0, y1 = sends
    x1 = swap(x1, "gx", 1)
    y1 = swap(y1, "gy", 1)
    x0 = swap(x0, "gx", 0)
    return x0, x1, swap(y0, "gy", 0), y1


def plus(one, two):
    return (one.astype(F32) + two.astype(F32)).astype(BF16)


def row_sum(keep, give):
    count = lax.axis_size("gy")
    one, two = keep, swap(give, "gy", 0)
    if count & (count - 1):
        part = plus(one, two)
        for step in range(2, count, 2):
            one, two = plus(one, two) if step > 2 else part, lax.ppermute(
                part, "gy", [(i, (i + step) % count) for i in range(count)]
            )
        return one, two
    step = 2
    while step < count:
        one = plus(one, two)
        two = lax.ppermute(one, "gy", [(i, i ^ step) for i in range(count)])
        step *= 2
    return one, two


def on_device(rhs, diag_blocks, inverse_blocks, couplings, prolong, face_source, subset):
    elements, dof, cols = rhs.shape
    fdof = couplings.shape[3]
    coarse = prolong.shape[1]
    groups = lax.axis_size("gy")
    half = elements // 2
    shape = jax.ShapeDtypeStruct
    state_s = shape((elements, dof, cols), F32)
    tr_s = shape((elements, 6, fdof, cols), BF16)
    sends_s = [shape((half, fdof, cols), BF16)] * 4
    y_s = shape((half, coarse, cols), BF16)
    near_rows = -(-2 * fdof // cols) * cols
    message = -(-(coarse + coarse // 2 + elements) // 16) * 16
    tmps = pltpu.VMEM((elements, 2, fdof, cols), F32)
    sides = pltpu.VMEM((4, half, fdof, cols), BF16)
    state_b = pltpu.VMEM((elements, dof, cols), BF16)
    square_b = pltpu.VMEM((elements, dof, dof), BF16)
    apply_flops = 2 * elements * dof * cols * (dof + 3 * fdof)
    inv_flops = 2 * elements * dof * dof * cols
    far_flops = 4 * elements * dof * fdof * cols
    coup = jnp.swapaxes(couplings, 2, 3)
    pt = prolong.T

    me = lax.axis_index("gy")
    spots = jnp.stack(
        [me, (me + groups - 1) % groups, (me + 1) % groups, lax.axis_index("gx")]
    ).astype(jnp.int32)
    first, tr, rhs, inv, *sends = run(
        first_body,
        (rhs, inverse_blocks, spots),
        [state_s, tr_s, shape(rhs.shape, BF16), shape(inverse_blocks.shape, BF16)] + sends_s,
        [tmps, sides, pltpu.SemaphoreType.DMA((2, elements))],
        inv_flops,
        far_ins=(0, 1),
    )
    xm, xp, ym, yp = exchange(sends)
    acc, mats, oper, outer, pf, wide = run(
        local_body,
        (rhs, first, diag_blocks, coup, tr, pt, face_source, subset),
        [
            state_s,
            shape((groups, coarse // 2, cols), F32),
            shape((elements, dof, 2 * dof), BF16),
            shape((elements, dof, near_rows), BF16),
            shape((6, fdof, cols), BF16),
            shape((dof, cols), BF16),
        ],
        [
            square_b,
            pltpu.VMEM(coup.shape, BF16),
            pltpu.VMEM((dof, cols), F32),
            pltpu.VMEM((2, fdof, cols), F32),
            pltpu.VMEM((groups, coarse, cols), F32),
            pltpu.SemaphoreType.DMA((2, elements)),
        ],
        2 * apply_flops,
        far_ins=(2, 3),
    )
    resid, keep, give = run(
        restrict_body,
        (acc, outer, xm, xp, ym, yp, pt, mats, face_source, subset, spots),
        [state_s] + [shape((groups // 2, message, cols), BF16)] * 2,
        [pltpu.VMEM((groups, coarse, cols), F32)],
        far_flops,
    )
    one, two = row_sum(keep, give)
    y_own, names = run(
        coarse_body,
        (one, two, spots),
        [shape((groups // 2, coarse, cols), BF16), shape((2, elements, cols), F32)],
        [],
        3 * groups * coarse * coarse * cols * CITER,
    )
    y_all, y0, y1 = run(
        choose_body,
        (y_own, swap(y_own, "gy", 0), subset, spots),
        [shape((groups, coarse, cols), BF16), y_s, y_s],
        [pltpu.VMEM((2, half, coarse, cols), BF16)],
        0,
    )
    y1 = swap(y1, "gx", 1)
    y0 = swap(y0, "gx", 0)
    acc, second = run(
        second_body,
        (resid, first, oper, outer, y_all, wide, pf, names, face_source, subset),
        [state_s, state_s],
        [],
        apply_flops,
    )
    state, tr, *sends = run(
        smooth_body,
        (acc, second, outer, inv, y0, y1, pf, face_source, spots),
        [state_s, tr_s] + sends_s,
        [tmps, sides, state_b],
        inv_flops,
    )
    xm, xp, ym, yp = exchange(sends)
    acc = run(inner_body, (rhs, state, oper, tr, face_source), [state_s], [], apply_flops)[0]
    return run(
        final_body,
        (acc, state, outer, inv, xm, xp, ym, yp, face_source, spots),
        [state_s],
        [state_b, pltpu.VMEM((elements, dof, cols), F32), pltpu.SemaphoreType.DMA((1, elements))],
        inv_flops + far_flops,
        far_outs=(0,),
    )[0]


def solution(mesh):
    return jax.shard_map(
        on_device,
        mesh=mesh,
        in_specs=(
            P(("gx", "gy"), None, None),
            P(("gx", "gy"), None, None),
            P(("gx", "gy"), None, None),
            P(("gx", "gy"), None, None, None),
            P(),
            P(("gx", "gy"), None),
            P(("gx", "gy")),
        ),
        out_specs=P(("gx", "gy"), None, None),
        check_vma=False,
    )
```

```python
import jax
import jax.numpy as jnp
from jax import lax
from jax.experimental import pallas as pl
from jax.experimental.pallas import tpu as pltpu
from jax.sharding import PartitionSpec as P

NVAR = 6
NP = 4
CITER = 4

relax_fine = 0.7
relax_coarse = 0.5

F32 = jnp.float32
BF16 = jnp.bfloat16
LIMIT = 24 * 1024 * 1024
PARTS = 2
OUT_PARTS = 8


def dot(a, b, precision=None):
    return jnp.dot(a, b, preferred_element_type=F32, precision=precision)


def place(e):
    return e % 2, e // 2 % 2, e // 4


def run(body, ins, outs, scratch, flops, far_ins=(), far_outs=()):
    size = sum(a.size * a.dtype.itemsize for a in list(ins) + list(outs))
    vmem = pl.BlockSpec(memory_space=pltpu.VMEM)
    smem = pl.BlockSpec(memory_space=pltpu.SMEM)
    hbm = pl.BlockSpec(memory_space=pltpu.HBM)
    ins = [
        pltpu.with_memory_space_constraint(a, pltpu.HBM) if n in far_ins else a
        for n, a in enumerate(ins)
    ]
    return pl.pallas_call(
        body,
        in_specs=[
            smem if a.dtype == jnp.int32 else hbm if n in far_ins else vmem
            for n, a in enumerate(ins)
        ],
        out_specs=[hbm if n in far_outs else vmem for n in range(len(outs))],
        out_shape=list(outs),
        scratch_shapes=scratch,
        compiler_params=pltpu.CompilerParams(vmem_limit_bytes=LIMIT),
        cost_estimate=pl.CostEstimate(flops=flops, bytes_accessed=size, transcendentals=0),
    )(*ins)


def chunks(count, pairs, sems, parts):
    size = count // parts
    return [
        [
            pltpu.make_async_copy(a.at[pl.ds(q * size, size)], b.at[pl.ds(q * size, size)], sems.at[n, q])
            for n, (a, b) in enumerate(pairs)
        ]
        for q in range(parts)
    ]


def read_traces(load, tmp):
    side = NP * NP
    layers = NVAR * NP
    faces = [load(0, layers * NP, NP), load(NP - 1, layers * NP, NP)]
    for g in (0, 1):
        for ii in range(NP):
            tmp[g, pl.ds(ii, layers, stride=NP), :] = load(g * NP * (NP - 1) + ii, layers, side)
        faces.append(tmp[g])
    for g in (0, 1):
        faces.append(
            jnp.concatenate(
                [load((v * NP + g * (NP - 1)) * side, side, 1) for v in range(NVAR)], axis=0
            )
        )
    return faces


def strided(ref):
    def load(start, size, stride):
        if stride == 1:
            return ref[pl.ds(start, size), :]
        return ref[pl.ds(start, size, stride=stride), :]

    return load


def emit_traces(e, state_ref, tr_ref, sides, tmp):
    faces = [f.astype(BF16) for f in read_traces(strided(state_ref.at[e]), tmp.at[e])]
    i, j, k = place(e)
    for f in (1 - i, 3 - j, 5 - k):
        tr_ref[e, f] = faces[f]
    sides[i, e // 2] = faces[i]
    sides[2 + j, i + 2 * k] = faces[2 + j]


def order(spots):
    return lax.rem(spots[3], 2) == 0, lax.rem(spots[0], 2) == 0


def pack_sends(spots, low, high, near, far):
    near[...] = jnp.where(spots, high, low)
    far[...] = jnp.where(spots, low, high)


def emit_sends(spots, sides, sends):
    for axis, even in enumerate(order(spots)):
        pack_sends(even, sides[2 * axis], sides[2 * axis + 1], sends[2 * axis], sends[2 * axis + 1])


def masked(face_source, e, f, value):
    return jnp.where(face_source[e, f] > 0, value, jnp.zeros_like(value))


def inner_faces(e):
    i, j, k = place(e)
    return (1 - i, e ^ 1, i), (3 - j, e ^ 2, 2 + j), (5 - k, e ^ 4, 4 + k)


def stack(parts, rows):
    have = sum(part.shape[0] for part in parts)
    if have < rows:
        parts = parts + [jnp.zeros((rows - have, parts[0].shape[1]), parts[0].dtype)]
    return jnp.concatenate(parts, axis=0)


def came(even, from_near, from_far, upper, at):
    first, second = (from_near, from_far) if upper else (from_far, from_near)
    return jnp.where(even, first[at], second[at])


def pick(e, halo, face_source, spots):
    i, j, k = place(e)
    even_x, even_y = order(spots)
    return [
        masked(face_source, e, i, came(even_x, halo[0], halo[1], i, e // 2)),
        masked(face_source, e, 2 + j, came(even_y, halo[2], halo[3], j, i + 2 * k)),
    ]


def first_body(
    rhs_far, inv_far, coup_far, spots,
    first, tr, rhs, inv, coup, s0, s1, s2, s3,
    tmp, sides, sems,
):
    count = rhs.shape[0]
    shares = chunks(count, ((inv_far, inv), (rhs_far, rhs)), sems, PARTS)
    later = pltpu.make_async_copy(coup_far, coup, sems.at[0, PARTS])
    for share in shares:
        for copy in share:
            copy.start()
    later.start()
    for e in range(count):
        if e % (count // PARTS) == 0:
            for copy in shares[e * PARTS // count]:
                copy.wait()
        first[e] = relax_fine * dot(inv[e], rhs[e])
        emit_traces(e, first, tr, sides, tmp)
    emit_sends(spots, sides, (s0, s1, s2, s3))
    later.wait()


def local_body(
    rhs, state, diag, coup, tr, pt, face_source, subset,
    acc, mats, oper, outer, pf, prolong,
    wide, tmp, msum,
):
    coarse, dof = pt.shape
    count, _, cols = acc.shape
    near_rows = outer.shape[2]
    wide[...] = stack([pt[...].astype(F32)], cols).T
    for f, face in enumerate(read_traces(strided(wide), tmp)):
        pf[f] = face.astype(BF16)
    base = wide[...].astype(BF16)
    prolong[...] = base
    msum[...] = jnp.zeros_like(msum)
    for e in range(count):
        i, j, k = place(e)
        inner = inner_faces(e)
        oper[e, :, 0:dof] = diag[e]
        oper[e, :, dof : 2 * dof] = stack([coup[e, f] for f, near, face in inner], dof).T
        outer[e] = stack([coup[e, i], coup[e, 2 + j]], near_rows).T
    stiffs = []
    for e in range(count):
        i, j, k = place(e)
        inner = inner_faces(e)
        values = [state[e].astype(BF16)] + [
            masked(face_source, e, f, tr[near, face]) for f, near, face in inner
        ]
        bases = [base] + [masked(face_source, e, f, pf[face]) for f, near, face in inner]
        both = jnp.concatenate([stack(values, 2 * dof), stack(bases, 2 * dof)], axis=1)
        total = dot(oper[e], both)
        acc[e] = rhs[e].astype(F32) - total[:, 0:cols]
        far = stack(
            [masked(face_source, e, i, pf[1 - i]), masked(face_source, e, 2 + j, pf[3 - j])],
            near_rows,
        )
        stiffs.append((total[:, cols:] + dot(outer[e], far)).astype(BF16))
    blocks = [dot(pt[...], stiff) for stiff in stiffs]
    lane = lax.broadcasted_iota(jnp.int32, (coarse, cols), 1)
    one = jnp.where(lane == coarse, 1.0, 0.0)
    for e in range(count):
        msum[subset[e]] += blocks[e] + one
    for s in range(mats.shape[0]):
        block = msum[s]
        low = jnp.where(lane == coarse, 0.0, block)[coarse // 2 :]
        mats[s] = block[: coarse // 2] + pltpu.roll(low, cols // 2, 1)


def restrict_body(part, outer, xm, xp, ym, yp, pt, mats, face_source, subset, spots, resid, keep, give, total):
    count = part.shape[0]
    coarse = pt.shape[0]
    total[...] = jnp.zeros_like(total)
    for e in range(count):
        far = stack(pick(e, (xm, xp, ym, yp), face_source, spots), outer.shape[2])
        resid[e] = part[e] - dot(outer[e], far)
    shares = [dot(pt[...], resid[e].astype(BF16)) for e in range(count)]
    for e in range(count):
        total[subset[e]] += shares[e]
    row = lax.broadcasted_iota(jnp.int32, (count, mats.shape[2]), 0)
    lane = lax.broadcasted_iota(jnp.int32, row.shape, 1)
    half = lax.rem(spots[0], 2)
    mine = (lane >= row.shape[1] // 2) == (half == 1)
    names = jnp.zeros(row.shape, F32)
    for e in range(count):
        names = jnp.where(mine & (row == e), subset[e].astype(F32), names)
    share = keep.shape[0]
    for which, ref in ((half, keep), (1 - half, give)):
        for s in range(share):
            own = jnp.where(lax.div(spots[0], 2) == s, names, 0.0)
            ref[s, 0:coarse] = total[which * share + s].astype(BF16)
            rest = stack([mats[which * share + s], own], ref.shape[1] - coarse)
            ref[s, coarse:] = rest.astype(BF16)


def split(value):
    high = value.astype(BF16)
    return high, (value - high.astype(F32)).astype(BF16)


def coarse_body(one, two, spots, y_own, names):
    groups, coarse, cols = y_own.shape
    half = coarse // 2
    rights, blocks, thetas, ys = [], [], [], []
    for s in range(groups):
        both = one[s].astype(F32) + two[s].astype(F32)
        right = both[0:coarse]
        packed = both[coarse : coarse + half]
        block = jnp.concatenate([packed, pltpu.roll(packed, cols // 2, 1)], axis=0)
        theta = relax_coarse / jnp.maximum(packed[:, coarse : coarse + 1], 1.0)
        theta = jnp.concatenate([theta, theta], axis=0)
        high, low = split(block[:, 0:coarse])
        rights.append(right)
        blocks.append(jnp.concatenate([high, high, low], axis=1))
        thetas.append(theta)
        ys.append(theta * right)
    for sweep in range(CITER - 1):
        sides = []
        for s in range(groups):
            high, low = split(ys[s])
            sides.append(jnp.concatenate([high, low, high], axis=0))
        applied = [dot(blocks[s], sides[s]) for s in range(groups)]
        ys = [ys[s] + thetas[s] * (rights[s] - applied[s]) for s in range(groups)]
    for s in range(groups):
        y_own[s] = ys[s].astype(BF16)
    start = coarse + half
    count = names.shape[1]
    lane = lax.broadcasted_iota(jnp.int32, (count, cols), 1)
    for side in (0, 1):
        slot = lax.div(spots[1 + side], 2)
        far = one[slot].astype(F32) + two[slot].astype(F32)
        mine = (lane >= cols // 2) == (lax.rem(spots[1 + side], 2) == 1)
        far = jnp.where(mine, far[start : start + count], 0.0)
        names[side] = far + pltpu.roll(far, cols // 2, 1)


def choose_body(y_own, y_other, subset, spots, y_all, near, far, sides):
    share = y_own.shape[0]
    half = lax.rem(spots[0], 2)
    for s in range(share):
        y_all[half * share + s] = y_own[s]
        y_all[(1 - half) * share + s] = y_other[s]
    for e in range(subset.shape[0]):
        sides[e % 2, e // 2] = y_all[subset[e]]
    pack_sends(order(spots)[0], sides[0], sides[1], near, far)


def second_body(resid, state, oper, outer, y_all, prolong, pf, names, face_source, subset, acc, second):
    coarse = y_all.shape[1]
    count, dof, _ = resid.shape
    inside, outside = [], []
    for e in range(count):
        i, j, k = place(e)
        step = dot(prolong[:, 0:coarse], y_all[subset[e]])
        second[e] = state[e] + step
        values = [step.astype(BF16)]
        for f, near, face in inner_faces(e):
            rows = dot(pf[face, :, 0:coarse], y_all[subset[near]]).astype(BF16)
            values.append(masked(face_source, e, f, rows))
        name = names[j, pl.ds(e ^ 2, 1), :]
        y_far = jnp.zeros(y_all.shape[1:], F32)
        for s in range(y_all.shape[0]):
            y_far = jnp.where(name == float(s), y_all[s].astype(F32), y_far)
        rows = dot(pf[3 - j, :, 0:coarse], y_far.astype(BF16)).astype(BF16)
        far = [jnp.zeros_like(rows), masked(face_source, e, 2 + j, rows)]
        inside.append(stack(values, 2 * dof))
        outside.append(stack(far, outer.shape[2]))
    for e in range(count):
        acc[e] = resid[e] - (dot(oper[e], inside[e]) + dot(outer[e], outside[e]))


def smooth_body(part, second, outer, inv, y0, y1, pf, face_source, spots, state, tr, s0, s1, s2, s3, tmp, sides, res):
    coarse = y0.shape[1]
    count = part.shape[0]
    rows = []
    for e in range(count):
        i = e % 2
        y_far = came(order(spots)[0], y0, y1, i, e // 2)
        value = dot(pf[1 - i, :, 0:coarse], y_far).astype(BF16)
        rows.append(stack([masked(face_source, e, i, value)], outer.shape[2]))
    for e in range(count):
        res[e] = (part[e] - dot(outer[e], rows[e])).astype(BF16)
    for e in range(count):
        state[e] = second[e] + relax_fine * dot(inv[e], res[e])
        emit_traces(e, state, tr, sides, tmp)
    emit_sends(spots, sides, (s0, s1, s2, s3))


def inner_body(rhs, state, oper, tr, face_source, acc):
    dof = state.shape[1]
    for e in range(state.shape[0]):
        values = [state[e].astype(BF16)] + [
            masked(face_source, e, f, tr[near, face]) for f, near, face in inner_faces(e)
        ]
        acc[e] = rhs[e].astype(F32) - dot(oper[e], stack(values, 2 * dof))


def final_body(part, state, outer, inv, xm, xp, ym, yp, face_source, spots, out_far, res, out, sems):
    count = state.shape[0]
    copies = chunks(count, ((out, out_far),), sems, OUT_PARTS)
    for e in range(count):
        far = stack(pick(e, (xm, xp, ym, yp), face_source, spots), outer.shape[2])
        res[e] = (part[e] - dot(outer[e], far)).astype(BF16)
    size = count // OUT_PARTS
    for e in range(count):
        out[e] = state[e] + relax_fine * dot(inv[e], res[e])
        if e % size == size - 1:
            copies[e // size][0].start()
    for (copy,) in copies:
        copy.wait()


def swap(value, axis, start):
    count = lax.axis_size(axis)
    pairs = [(i % count, (i + 1) % count) for i in range(start, count, 2)]
    return lax.ppermute(value, axis, pairs + [(b, a) for a, b in pairs])


def exchange(sends):
    x0, x1, y0, y1 = sends
    x1 = swap(x1, "gx", 1)
    y1 = swap(y1, "gy", 1)
    x0 = swap(x0, "gx", 0)
    return x0, x1, swap(y0, "gy", 0), y1


def plus(one, two):
    return (one.astype(F32) + two.astype(F32)).astype(BF16)


def row_sum(keep, give):
    count = lax.axis_size("gy")
    one, two = keep, swap(give, "gy", 0)
    if count & (count - 1):
        part = plus(one, two)
        for step in range(2, count, 2):
            one, two = plus(one, two) if step > 2 else part, lax.ppermute(
                part, "gy", [(i, (i + step) % count) for i in range(count)]
            )
        return one, two
    step = 2
    while step < count:
        one = plus(one, two)
        two = lax.ppermute(one, "gy", [(i, i ^ step) for i in range(count)])
        step *= 2
    return one, two


def on_device(rhs, diag_blocks, inverse_blocks, couplings, prolong, face_source, subset):
    elements, dof, cols = rhs.shape
    fdof = couplings.shape[3]
    coarse = prolong.shape[1]
    groups = lax.axis_size("gy")
    half = elements // 2
    shape = jax.ShapeDtypeStruct
    state_s = shape((elements, dof, cols), F32)
    tr_s = shape((elements, 6, fdof, cols), BF16)
    sends_s = [shape((half, fdof, cols), BF16)] * 4
    y_s = shape((half, coarse, cols), BF16)
    near_rows = -(-2 * fdof // cols) * cols
    message = -(-(coarse + coarse // 2 + elements) // 16) * 16
    tmps = pltpu.VMEM((elements, 2, fdof, cols), F32)
    sides = pltpu.VMEM((4, half, fdof, cols), BF16)
    state_b = pltpu.VMEM((elements, dof, cols), BF16)
    apply_flops = 2 * elements * dof * cols * (dof + 3 * fdof)
    inv_flops = 2 * elements * dof * dof * cols
    far_flops = 4 * elements * dof * fdof * cols
    coup = jnp.swapaxes(couplings, 2, 3)
    pt = prolong.T

    me = lax.axis_index("gy")
    spots = jnp.stack(
        [me, (me + groups - 1) % groups, (me + 1) % groups, lax.axis_index("gx")]
    ).astype(jnp.int32)
    first, tr, rhs, inv, coup, *sends = run(
        first_body,
        (rhs, inverse_blocks, coup, spots),
        [state_s, tr_s] + [shape(a.shape, BF16) for a in (rhs, inverse_blocks, coup)] + sends_s,
        [tmps, sides, pltpu.SemaphoreType.DMA((2, PARTS + 1))],
        inv_flops,
        far_ins=(0, 1, 2),
    )
    xm, xp, ym, yp = exchange(sends)
    acc, mats, oper, outer, pf, wide = run(
        local_body,
        (rhs, first, diag_blocks, coup, tr, pt, face_source, subset),
        [
            state_s,
            shape((groups, coarse // 2, cols), F32),
            shape((elements, dof, 2 * dof), BF16),
            shape((elements, dof, near_rows), BF16),
            shape((6, fdof, cols), BF16),
            shape((dof, cols), BF16),
        ],
        [
            pltpu.VMEM((dof, cols), F32),
            pltpu.VMEM((2, fdof, cols), F32),
            pltpu.VMEM((groups, coarse, cols), F32),
        ],
        2 * apply_flops,
    )
    resid, keep, give = run(
        restrict_body,
        (acc, outer, xm, xp, ym, yp, pt, mats, face_source, subset, spots),
        [state_s] + [shape((groups // 2, message, cols), BF16)] * 2,
        [pltpu.VMEM((groups, coarse, cols), F32)],
        far_flops,
    )
    one, two = row_sum(keep, give)
    y_own, names = run(
        coarse_body,
        (one, two, spots),
        [shape((groups // 2, coarse, cols), BF16), shape((2, elements, cols), F32)],
        [],
        3 * groups * coarse * coarse * cols * CITER,
    )
    y_all, y0, y1 = run(
        choose_body,
        (y_own, swap(y_own, "gy", 0), subset, spots),
        [shape((groups, coarse, cols), BF16), y_s, y_s],
        [pltpu.VMEM((2, half, coarse, cols), BF16)],
        0,
    )
    y1 = swap(y1, "gx", 1)
    y0 = swap(y0, "gx", 0)
    acc, second = run(
        second_body,
        (resid, first, oper, outer, y_all, wide, pf, names, face_source, subset),
        [state_s, state_s],
        [],
        apply_flops,
    )
    state, tr, *sends = run(
        smooth_body,
        (acc, second, outer, inv, y0, y1, pf, face_source, spots),
        [state_s, tr_s] + sends_s,
        [tmps, sides, state_b],
        inv_flops,
    )
    xm, xp, ym, yp = exchange(sends)
    acc = run(inner_body, (rhs, state, oper, tr, face_source), [state_s], [], apply_flops)[0]
    return run(
        final_body,
        (acc, state, outer, inv, xm, xp, ym, yp, face_source, spots),
        [state_s],
        [state_b, pltpu.VMEM((elements, dof, cols), F32), pltpu.SemaphoreType.DMA((1, elements))],
        inv_flops + far_flops,
        far_outs=(0,),
    )[0]


def solution(mesh):
    return jax.shard_map(
        on_device,
        mesh=mesh,
        in_specs=(
            P(("gx", "gy"), None, None),
            P(("gx", "gy"), None, None),
            P(("gx", "gy"), None, None),
            P(("gx", "gy"), None, None, None),
            P(),
            P(("gx", "gy"), None),
            P(("gx", "gy")),
        ),
        out_specs=P(("gx", "gy"), None, None),
        check_vma=False,
    )
```

```python
import jax
import jax.numpy as jnp
from jax import lax
from jax.experimental import pallas as pl
from jax.experimental.pallas import tpu as pltpu
from jax.sharding import PartitionSpec as P

NVAR = 6
NP = 4
CITER = 4

relax_fine = 0.7
relax_coarse = 0.5

F32 = jnp.float32
BF16 = jnp.bfloat16
LIMIT = 24 * 1024 * 1024
PARTS = 2
OUT_PARTS = 8


def dot(a, b, precision=None):
    return jnp.dot(a, b, preferred_element_type=F32, precision=precision)


def place(e):
    return e % 2, e // 2 % 2, e // 4


def run(body, ins, outs, scratch, flops, far_ins=(), far_outs=()):
    size = sum(a.size * a.dtype.itemsize for a in list(ins) + list(outs))
    vmem = pl.BlockSpec(memory_space=pltpu.VMEM)
    smem = pl.BlockSpec(memory_space=pltpu.SMEM)
    hbm = pl.BlockSpec(memory_space=pltpu.HBM)
    ins = [
        pltpu.with_memory_space_constraint(a, pltpu.HBM) if n in far_ins else a
        for n, a in enumerate(ins)
    ]
    return pl.pallas_call(
        body,
        in_specs=[
            smem if a.dtype == jnp.int32 else hbm if n in far_ins else vmem
            for n, a in enumerate(ins)
        ],
        out_specs=[hbm if n in far_outs else vmem for n in range(len(outs))],
        out_shape=list(outs),
        scratch_shapes=scratch,
        compiler_params=pltpu.CompilerParams(vmem_limit_bytes=LIMIT),
        cost_estimate=pl.CostEstimate(flops=flops, bytes_accessed=size, transcendentals=0),
    )(*ins)


def chunks(count, pairs, sems, parts):
    size = count // parts
    return [
        [
            pltpu.make_async_copy(a.at[pl.ds(q * size, size)], b.at[pl.ds(q * size, size)], sems.at[n, q])
            for n, (a, b) in enumerate(pairs)
        ]
        for q in range(parts)
    ]


def read_traces(load, tmp):
    side = NP * NP
    layers = NVAR * NP
    faces = [load(0, layers * NP, NP), load(NP - 1, layers * NP, NP)]
    for g in (0, 1):
        for ii in range(NP):
            tmp[g, pl.ds(ii, layers, stride=NP), :] = load(g * NP * (NP - 1) + ii, layers, side)
        faces.append(tmp[g])
    for g in (0, 1):
        faces.append(
            jnp.concatenate(
                [load((v * NP + g * (NP - 1)) * side, side, 1) for v in range(NVAR)], axis=0
            )
        )
    return faces


def strided(ref):
    def load(start, size, stride):
        if stride == 1:
            return ref[pl.ds(start, size), :]
        return ref[pl.ds(start, size, stride=stride), :]

    return load


def emit_traces(e, state_ref, tr_ref, sides, tmp):
    faces = [f.astype(BF16) for f in read_traces(strided(state_ref.at[e]), tmp.at[e])]
    i, j, k = place(e)
    for f in (1 - i, 3 - j, 5 - k):
        tr_ref[e, f] = faces[f]
    sides[i, e // 2] = faces[i]
    sides[2 + j, i + 2 * k] = faces[2 + j]


def order(spots):
    return lax.rem(spots[3], 2) == 0, lax.rem(spots[0], 2) == 0


def pack_sends(spots, low, high, near, far):
    near[...] = jnp.where(spots, high, low)
    far[...] = jnp.where(spots, low, high)


def emit_sends(spots, sides, sends):
    for axis, even in enumerate(order(spots)):
        pack_sends(even, sides[2 * axis], sides[2 * axis + 1], sends[2 * axis], sends[2 * axis + 1])


def masked(face_source, e, f, value):
    return jnp.where(face_source[e, f] > 0, value, jnp.zeros_like(value))


def inner_faces(e):
    i, j, k = place(e)
    return (1 - i, e ^ 1, i), (3 - j, e ^ 2, 2 + j), (5 - k, e ^ 4, 4 + k)


def stack(parts, rows):
    have = sum(part.shape[0] for part in parts)
    if have < rows:
        parts = parts + [jnp.zeros((rows - have, parts[0].shape[1]), parts[0].dtype)]
    return jnp.concatenate(parts, axis=0)


def came(even, from_near, from_far, upper, at):
    first, second = (from_near, from_far) if upper else (from_far, from_near)
    return jnp.where(even, first[at], second[at])


def pick(e, halo, face_source, spots):
    i, j, k = place(e)
    even_x, even_y = order(spots)
    return [
        masked(face_source, e, i, came(even_x, halo[0], halo[1], i, e // 2)),
        masked(face_source, e, 2 + j, came(even_y, halo[2], halo[3], j, i + 2 * k)),
    ]


def first_body(
    rhs_far, inv_far, coup_far, spots,
    first, tr, rhs, inv, coup, s0, s1, s2, s3,
    tmp, sides, sems,
):
    count = rhs.shape[0]
    shares = chunks(count, ((inv_far, inv), (rhs_far, rhs)), sems, PARTS)
    later = pltpu.make_async_copy(coup_far, coup, sems.at[0, PARTS])
    for share in shares:
        for copy in share:
            copy.start()
    later.start()
    for e in range(count):
        if e % (count // PARTS) == 0:
            for copy in shares[e * PARTS // count]:
                copy.wait()
        first[e] = relax_fine * dot(inv[e], rhs[e])
        emit_traces(e, first, tr, sides, tmp)
    emit_sends(spots, sides, (s0, s1, s2, s3))
    later.wait()


def local_body(
    rhs, state, diag, coup, tr, pt, face_source, subset,
    acc, mats, oper, outer, pf, prolong,
    wide, tmp, msum,
):
    coarse, dof = pt.shape
    count, _, cols = acc.shape
    near_rows = outer.shape[2]
    wide[...] = stack([pt[...].astype(F32)], cols).T
    for f, face in enumerate(read_traces(strided(wide), tmp)):
        pf[f] = face.astype(BF16)
    base = wide[...].astype(BF16)
    prolong[...] = base
    msum[...] = jnp.zeros_like(msum)
    for e in range(count):
        i, j, k = place(e)
        inner = inner_faces(e)
        oper[e, :, 0:dof] = diag[e]
        oper[e, :, dof : 2 * dof] = stack([coup[e, f] for f, near, face in inner], dof).T
        outer[e] = stack([coup[e, i], coup[e, 2 + j]], near_rows).T
    stiffs = []
    for e in range(count):
        i, j, k = place(e)
        inner = inner_faces(e)
        values = [state[e].astype(BF16)] + [
            masked(face_source, e, f, tr[near, face]) for f, near, face in inner
        ]
        bases = [base] + [masked(face_source, e, f, pf[face]) for f, near, face in inner]
        both = jnp.concatenate([stack(values, 2 * dof), stack(bases, 2 * dof)], axis=1)
        total = dot(oper[e], both)
        acc[e] = rhs[e].astype(F32) - total[:, 0:cols]
        far = stack(
            [masked(face_source, e, i, pf[1 - i]), masked(face_source, e, 2 + j, pf[3 - j])],
            near_rows,
        )
        stiffs.append((total[:, cols:] + dot(outer[e], far)).astype(BF16))
    blocks = [dot(pt[...], stiff) for stiff in stiffs]
    lane = lax.broadcasted_iota(jnp.int32, (coarse, cols), 1)
    one = jnp.where(lane == coarse, 1.0, 0.0)
    for e in range(count):
        msum[subset[e]] += blocks[e] + one
    for s in range(mats.shape[0]):
        block = msum[s]
        low = jnp.where(lane == coarse, 0.0, block)[coarse // 2 :]
        mats[s] = block[: coarse // 2] + pltpu.roll(low, cols // 2, 1)


def restrict_body(part, outer, xp, yp, xm, ym, pt, mats, face_source, subset, spots, resid, keep, give, total):
    count = part.shape[0]
    coarse = pt.shape[0]
    total[...] = jnp.zeros_like(total)
    for e in range(count):
        far = stack(pick(e, (xm, xp, ym, yp), face_source, spots), outer.shape[2])
        resid[e] = part[e] - dot(outer[e], far)
    shares = [dot(pt[...], resid[e].astype(BF16)) for e in range(count)]
    for e in range(count):
        total[subset[e]] += shares[e]
    row = lax.broadcasted_iota(jnp.int32, (count, mats.shape[2]), 0)
    lane = lax.broadcasted_iota(jnp.int32, row.shape, 1)
    half = lax.rem(spots[0], 2)
    mine = (lane >= row.shape[1] // 2) == (half == 1)
    names = jnp.zeros(row.shape, F32)
    for e in range(count):
        names = jnp.where(mine & (row == e), subset[e].astype(F32), names)
    share = keep.shape[0]
    for which, ref in ((half, keep), (1 - half, give)):
        for s in range(share):
            own = jnp.where(lax.div(spots[0], 2) == s, names, 0.0)
            ref[s, 0:coarse] = total[which * share + s].astype(BF16)
            rest = stack([mats[which * share + s], own], ref.shape[1] - coarse)
            ref[s, coarse:] = rest.astype(BF16)


def split(value):
    high = value.astype(BF16)
    return high, (value - high.astype(F32)).astype(BF16)


def coarse_body(one, two, spots, y_own, names):
    groups, coarse, cols = y_own.shape
    half = coarse // 2
    rights, blocks, thetas, ys = [], [], [], []
    for s in range(groups):
        both = one[s].astype(F32) + two[s].astype(F32)
        right = both[0:coarse]
        packed = both[coarse : coarse + half]
        block = jnp.concatenate([packed, pltpu.roll(packed, cols // 2, 1)], axis=0)
        theta = relax_coarse / jnp.maximum(packed[:, coarse : coarse + 1], 1.0)
        theta = jnp.concatenate([theta, theta], axis=0)
        high, low = split(block[:, 0:coarse])
        rights.append(right)
        blocks.append(jnp.concatenate([high, high, low], axis=1))
        thetas.append(theta)
        ys.append(theta * right)
    for sweep in range(CITER - 1):
        sides = []
        for s in range(groups):
            high, low = split(ys[s])
            sides.append(jnp.concatenate([high, low, high], axis=0))
        applied = [dot(blocks[s], sides[s]) for s in range(groups)]
        ys = [ys[s] + thetas[s] * (rights[s] - applied[s]) for s in range(groups)]
    for s in range(groups):
        y_own[s] = ys[s].astype(BF16)
    start = coarse + half
    count = names.shape[1]
    lane = lax.broadcasted_iota(jnp.int32, (count, cols), 1)
    for side in (0, 1):
        slot = lax.div(spots[1 + side], 2)
        far = one[slot].astype(F32) + two[slot].astype(F32)
        mine = (lane >= cols // 2) == (lax.rem(spots[1 + side], 2) == 1)
        far = jnp.where(mine, far[start : start + count], 0.0)
        names[side] = far + pltpu.roll(far, cols // 2, 1)


def choose_body(y_own, y_other, subset, spots, y_all, near, far, sides):
    share = y_own.shape[0]
    half = lax.rem(spots[0], 2)
    for s in range(share):
        y_all[half * share + s] = y_own[s]
        y_all[(1 - half) * share + s] = y_other[s]
    for e in range(subset.shape[0]):
        sides[e % 2, e // 2] = y_all[subset[e]]
    pack_sends(order(spots)[0], sides[0], sides[1], near, far)


def second_body(resid, state, oper, outer, y_all, prolong, pf, names, face_source, subset, acc, second):
    coarse = y_all.shape[1]
    count, dof, _ = resid.shape
    inside, outside = [], []
    for e in range(count):
        i, j, k = place(e)
        step = dot(prolong[:, 0:coarse], y_all[subset[e]])
        second[e] = state[e] + step
        values = [step.astype(BF16)]
        for f, near, face in inner_faces(e):
            rows = dot(pf[face, :, 0:coarse], y_all[subset[near]]).astype(BF16)
            values.append(masked(face_source, e, f, rows))
        name = names[j, pl.ds(e ^ 2, 1), :]
        y_far = jnp.zeros(y_all.shape[1:], F32)
        for s in range(y_all.shape[0]):
            y_far = jnp.where(name == float(s), y_all[s].astype(F32), y_far)
        rows = dot(pf[3 - j, :, 0:coarse], y_far.astype(BF16)).astype(BF16)
        far = [jnp.zeros_like(rows), masked(face_source, e, 2 + j, rows)]
        inside.append(stack(values, 2 * dof))
        outside.append(stack(far, outer.shape[2]))
    for e in range(count):
        acc[e] = resid[e] - (dot(oper[e], inside[e]) + dot(outer[e], outside[e]))


def smooth_body(part, second, outer, inv, y1, y0, pf, face_source, spots, state, tr, s0, s1, s2, s3, tmp, sides, res):
    coarse = y0.shape[1]
    count = part.shape[0]
    rows = []
    for e in range(count):
        i = e % 2
        y_far = came(order(spots)[0], y0, y1, i, e // 2)
        value = dot(pf[1 - i, :, 0:coarse], y_far).astype(BF16)
        rows.append(stack([masked(face_source, e, i, value)], outer.shape[2]))
    for e in range(count):
        res[e] = (part[e] - dot(outer[e], rows[e])).astype(BF16)
    for e in range(count):
        state[e] = second[e] + relax_fine * dot(inv[e], res[e])
        emit_traces(e, state, tr, sides, tmp)
    emit_sends(spots, sides, (s0, s1, s2, s3))


def inner_body(rhs, state, oper, tr, face_source, acc):
    dof = state.shape[1]
    for e in range(state.shape[0]):
        values = [state[e].astype(BF16)] + [
            masked(face_source, e, f, tr[near, face]) for f, near, face in inner_faces(e)
        ]
        acc[e] = rhs[e].astype(F32) - dot(oper[e], stack(values, 2 * dof))


def final_body(part, state, outer, inv, xp, yp, xm, ym, face_source, spots, out_far, res, out, sems):
    count = state.shape[0]
    copies = chunks(count, ((out, out_far),), sems, OUT_PARTS)
    for e in range(count):
        far = stack(pick(e, (xm, xp, ym, yp), face_source, spots), outer.shape[2])
        res[e] = (part[e] - dot(outer[e], far)).astype(BF16)
    size = count // OUT_PARTS
    for e in range(count):
        out[e] = state[e] + relax_fine * dot(inv[e], res[e])
        if e % size == size - 1:
            copies[e // size][0].start()
    for (copy,) in copies:
        copy.wait()


def swap(value, axis, start):
    count = lax.axis_size(axis)
    pairs = [(i % count, (i + 1) % count) for i in range(start, count, 2)]
    return lax.ppermute(value, axis, pairs + [(b, a) for a, b in pairs])


def exchange(sends):
    x0, x1, y0, y1 = sends
    x1 = swap(x1, "gx", 1)
    y1 = swap(y1, "gy", 1)
    x0 = swap(x0, "gx", 0)
    y0 = swap(y0, "gy", 0)
    return x0, x1, y0, y1


def plus(one, two):
    return (one.astype(F32) + two.astype(F32)).astype(BF16)


def row_sum(keep, give):
    count = lax.axis_size("gy")
    one, two = keep, swap(give, "gy", 0)
    if count & (count - 1):
        part = plus(one, two)
        for step in range(2, count, 2):
            one, two = plus(one, two) if step > 2 else part, lax.ppermute(
                part, "gy", [(i, (i + step) % count) for i in range(count)]
            )
        return one, two
    step = 2
    while step < count:
        one = plus(one, two)
        two = lax.ppermute(one, "gy", [(i, i ^ step) for i in range(count)])
        step *= 2
    return one, two


def on_device(rhs, diag_blocks, inverse_blocks, couplings, prolong, face_source, subset):
    elements, dof, cols = rhs.shape
    fdof = couplings.shape[3]
    coarse = prolong.shape[1]
    groups = lax.axis_size("gy")
    half = elements // 2
    shape = jax.ShapeDtypeStruct
    state_s = shape((elements, dof, cols), F32)
    tr_s = shape((elements, 6, fdof, cols), BF16)
    sends_s = [shape((half, fdof, cols), BF16)] * 4
    y_s = shape((half, coarse, cols), BF16)
    near_rows = -(-2 * fdof // cols) * cols
    message = -(-(coarse + coarse // 2 + elements) // 16) * 16
    tmps = pltpu.VMEM((elements, 2, fdof, cols), F32)
    sides = pltpu.VMEM((4, half, fdof, cols), BF16)
    state_b = pltpu.VMEM((elements, dof, cols), BF16)
    apply_flops = 2 * elements * dof * cols * (dof + 3 * fdof)
    inv_flops = 2 * elements * dof * dof * cols
    far_flops = 4 * elements * dof * fdof * cols
    coup = jnp.swapaxes(couplings, 2, 3)
    pt = prolong.T

    me = lax.axis_index("gy")
    spots = jnp.stack(
        [me, (me + groups - 1) % groups, (me + 1) % groups, lax.axis_index("gx")]
    ).astype(jnp.int32)
    first, tr, rhs, inv, coup, *sends = run(
        first_body,
        (rhs, inverse_blocks, coup, spots),
        [state_s, tr_s] + [shape(a.shape, BF16) for a in (rhs, inverse_blocks, coup)] + sends_s,
        [tmps, sides, pltpu.SemaphoreType.DMA((2, PARTS + 1))],
        inv_flops,
        far_ins=(0, 1, 2),
    )
    xm, xp, ym, yp = exchange(sends)
    acc, mats, oper, outer, pf, wide = run(
        local_body,
        (rhs, first, diag_blocks, coup, tr, pt, face_source, subset),
        [
            state_s,
            shape((groups, coarse // 2, cols), F32),
            shape((elements, dof, 2 * dof), BF16),
            shape((elements, dof, near_rows), BF16),
            shape((6, fdof, cols), BF16),
            shape((dof, cols), BF16),
        ],
        [
            pltpu.VMEM((dof, cols), F32),
            pltpu.VMEM((2, fdof, cols), F32),
            pltpu.VMEM((groups, coarse, cols), F32),
        ],
        2 * apply_flops,
    )
    resid, keep, give = run(
        restrict_body,
        (acc, outer, xp, yp, xm, ym, pt, mats, face_source, subset, spots),
        [state_s] + [shape((groups // 2, message, cols), BF16)] * 2,
        [pltpu.VMEM((groups, coarse, cols), F32)],
        far_flops,
    )
    one, two = row_sum(keep, give)
    y_own, names = run(
        coarse_body,
        (one, two, spots),
        [shape((groups // 2, coarse, cols), BF16), shape((2, elements, cols), F32)],
        [],
        3 * groups * coarse * coarse * cols * CITER,
    )
    y_all, y0, y1 = run(
        choose_body,
        (y_own, swap(y_own, "gy", 0), subset, spots),
        [shape((groups, coarse, cols), BF16), y_s, y_s],
        [pltpu.VMEM((2, half, coarse, cols), BF16)],
        0,
    )
    y1 = swap(y1, "gx", 1)
    y0 = swap(y0, "gx", 0)
    acc, second = run(
        second_body,
        (resid, first, oper, outer, y_all, wide, pf, names, face_source, subset),
        [state_s, state_s],
        [],
        apply_flops,
    )
    state, tr, *sends = run(
        smooth_body,
        (acc, second, outer, inv, y1, y0, pf, face_source, spots),
        [state_s, tr_s] + sends_s,
        [tmps, sides, state_b],
        inv_flops,
    )
    xm, xp, ym, yp = exchange(sends)
    acc = run(inner_body, (rhs, state, oper, tr, face_source), [state_s], [], apply_flops)[0]
    return run(
        final_body,
        (acc, state, outer, inv, xp, yp, xm, ym, face_source, spots),
        [state_s],
        [state_b, pltpu.VMEM((elements, dof, cols), F32), pltpu.SemaphoreType.DMA((1, elements))],
        inv_flops + far_flops,
        far_outs=(0,),
    )[0]


def solution(mesh):
    return jax.shard_map(
        on_device,
        mesh=mesh,
        in_specs=(
            P(("gx", "gy"), None, None),
            P(("gx", "gy"), None, None),
            P(("gx", "gy"), None, None),
            P(("gx", "gy"), None, None, None),
            P(),
            P(("gx", "gy"), None),
            P(("gx", "gy")),
        ),
        out_specs=P(("gx", "gy"), None, None),
        check_vma=False,
    )
```

```python
import jax
import jax.numpy as jnp
from jax import lax
from jax.experimental import pallas as pl
from jax.experimental.pallas import tpu as pltpu
from jax.sharding import PartitionSpec as P

NVAR = 6
NP = 4
CITER = 4

relax_fine = 0.7
relax_coarse = 0.5

F32 = jnp.float32
BF16 = jnp.bfloat16
LIMIT = 24 * 1024 * 1024
PARTS = 2
OUT_PARTS = 8


def dot(a, b, precision=None):
    return jnp.dot(a, b, preferred_element_type=F32, precision=precision)


def place(e):
    return e % 2, e // 2 % 2, e // 4


def run(body, ins, outs, scratch, flops, far_ins=(), far_outs=()):
    size = sum(a.size * a.dtype.itemsize for a in list(ins) + list(outs))
    vmem = pl.BlockSpec(memory_space=pltpu.VMEM)
    smem = pl.BlockSpec(memory_space=pltpu.SMEM)
    hbm = pl.BlockSpec(memory_space=pltpu.HBM)
    ins = [
        pltpu.with_memory_space_constraint(a, pltpu.HBM) if n in far_ins else a
        for n, a in enumerate(ins)
    ]
    return pl.pallas_call(
        body,
        in_specs=[
            smem if a.dtype == jnp.int32 else hbm if n in far_ins else vmem
            for n, a in enumerate(ins)
        ],
        out_specs=[hbm if n in far_outs else vmem for n in range(len(outs))],
        out_shape=list(outs),
        scratch_shapes=scratch,
        compiler_params=pltpu.CompilerParams(vmem_limit_bytes=LIMIT),
        cost_estimate=pl.CostEstimate(flops=flops, bytes_accessed=size, transcendentals=0),
    )(*ins)


def chunks(count, pairs, sems, parts):
    size = count // parts
    return [
        [
            pltpu.make_async_copy(a.at[pl.ds(q * size, size)], b.at[pl.ds(q * size, size)], sems.at[n, q])
            for n, (a, b) in enumerate(pairs)
        ]
        for q in range(parts)
    ]


def read_traces(load, tmp):
    side = NP * NP
    layers = NVAR * NP
    faces = [load(0, layers * NP, NP), load(NP - 1, layers * NP, NP)]
    for g in (0, 1):
        for ii in range(NP):
            tmp[g, pl.ds(ii, layers, stride=NP), :] = load(g * NP * (NP - 1) + ii, layers, side)
        faces.append(tmp[g])
    for g in (0, 1):
        faces.append(
            jnp.concatenate(
                [load((v * NP + g * (NP - 1)) * side, side, 1) for v in range(NVAR)], axis=0
            )
        )
    return faces


def strided(ref):
    def load(start, size, stride):
        if stride == 1:
            return ref[pl.ds(start, size), :]
        return ref[pl.ds(start, size, stride=stride), :]

    return load


def emit_traces(e, state_ref, tr_ref, sides, tmp):
    faces = [f.astype(BF16) for f in read_traces(strided(state_ref.at[e]), tmp.at[e])]
    i, j, k = place(e)
    for f in (1 - i, 3 - j, 5 - k):
        tr_ref[e, f] = faces[f]
    sides[i, e // 2] = faces[i]
    sides[2 + j, i + 2 * k] = faces[2 + j]


def order(spots):
    return lax.rem(spots[3], 2) == 0, lax.rem(spots[0], 2) == 0


def pack_sends(spots, low, high, near, far):
    near[...] = jnp.where(spots, high, low)
    far[...] = jnp.where(spots, low, high)


def emit_sends(spots, sides, sends):
    for axis, even in enumerate(order(spots)):
        pack_sends(even, sides[2 * axis], sides[2 * axis + 1], sends[2 * axis], sends[2 * axis + 1])


def masked(face_source, e, f, value):
    return jnp.where(face_source[e, f] > 0, value, jnp.zeros_like(value))


def inner_faces(e):
    i, j, k = place(e)
    return (1 - i, e ^ 1, i), (3 - j, e ^ 2, 2 + j), (5 - k, e ^ 4, 4 + k)


def stack(parts, rows):
    have = sum(part.shape[0] for part in parts)
    if have < rows:
        parts = parts + [jnp.zeros((rows - have, parts[0].shape[1]), parts[0].dtype)]
    return jnp.concatenate(parts, axis=0)


def came(even, from_near, from_far, upper, at):
    first, second = (from_near, from_far) if upper else (from_far, from_near)
    return jnp.where(even, first[at], second[at])


def pick(e, halo, face_source, spots):
    i, j, k = place(e)
    even_x, even_y = order(spots)
    return [
        masked(face_source, e, i, came(even_x, halo[0], halo[1], i, e // 2)),
        masked(face_source, e, 2 + j, came(even_y, halo[2], halo[3], j, i + 2 * k)),
    ]


def first_body(
    rhs_far, inv_far, coup_far, spots,
    first, tr, rhs, inv, coup, s0, s1, s2, s3,
    tmp, sides, sems,
):
    count = rhs.shape[0]
    shares = chunks(count, ((inv_far, inv), (rhs_far, rhs)), sems, PARTS)
    later = pltpu.make_async_copy(coup_far, coup, sems.at[0, PARTS])
    for share in shares:
        for copy in share:
            copy.start()
    later.start()
    for e in range(count):
        if e % (count // PARTS) == 0:
            for copy in shares[e * PARTS // count]:
                copy.wait()
        first[e] = relax_fine * dot(inv[e], rhs[e])
        emit_traces(e, first, tr, sides, tmp)
    emit_sends(spots, sides, (s0, s1, s2, s3))
    later.wait()


def local_body(
    rhs, state, diag, coup, tr, pt, face_source, subset,
    acc, mats, oper, outer, pf, prolong,
    wide, tmp, msum,
):
    coarse, dof = pt.shape
    count, _, cols = acc.shape
    near_rows = outer.shape[2]
    wide[...] = stack([pt[...].astype(F32)], cols).T
    for f, face in enumerate(read_traces(strided(wide), tmp)):
        pf[f] = face.astype(BF16)
    base = wide[...].astype(BF16)
    prolong[...] = base
    msum[...] = jnp.zeros_like(msum)
    for e in range(count):
        i, j, k = place(e)
        inner = inner_faces(e)
        oper[e, :, 0:dof] = diag[e]
        oper[e, :, dof : 2 * dof] = stack([coup[e, f] for f, near, face in inner], dof).T
        outer[e] = stack([coup[e, i], coup[e, 2 + j]], near_rows).T
    stiffs = []
    for e in range(count):
        i, j, k = place(e)
        inner = inner_faces(e)
        values = [state[e].astype(BF16)] + [
            masked(face_source, e, f, tr[near, face]) for f, near, face in inner
        ]
        bases = [base] + [masked(face_source, e, f, pf[face]) for f, near, face in inner]
        both = jnp.concatenate([stack(values, 2 * dof), stack(bases, 2 * dof)], axis=1)
        total = dot(oper[e], both)
        acc[e] = rhs[e].astype(F32) - total[:, 0:cols]
        far = stack(
            [masked(face_source, e, i, pf[1 - i]), masked(face_source, e, 2 + j, pf[3 - j])],
            near_rows,
        )
        stiffs.append((total[:, cols:] + dot(outer[e], far)).astype(BF16))
    blocks = [dot(pt[...], stiff) for stiff in stiffs]
    lane = lax.broadcasted_iota(jnp.int32, (coarse, cols), 1)
    one = jnp.where(lane == coarse, 1.0, 0.0)
    for e in range(count):
        msum[subset[e]] += blocks[e] + one
    for s in range(mats.shape[0]):
        block = msum[s]
        low = jnp.where(lane == coarse, 0.0, block)[coarse // 2 :]
        mats[s] = block[: coarse // 2] + pltpu.roll(low, cols // 2, 1)


def restrict_body(part, outer, xp, yp, xm, ym, pt, mats, face_source, subset, spots, resid, keep, give, total):
    count = part.shape[0]
    coarse = pt.shape[0]
    total[...] = jnp.zeros_like(total)
    for e in range(count):
        far = stack(pick(e, (xm, xp, ym, yp), face_source, spots), outer.shape[2])
        resid[e] = part[e] - dot(outer[e], far)
    shares = [dot(pt[...], resid[e].astype(BF16)) for e in range(count)]
    for e in range(count):
        total[subset[e]] += shares[e]
    row = lax.broadcasted_iota(jnp.int32, (count, mats.shape[2]), 0)
    lane = lax.broadcasted_iota(jnp.int32, row.shape, 1)
    half = lax.rem(spots[0], 2)
    mine = (lane >= row.shape[1] // 2) == (half == 1)
    names = jnp.zeros(row.shape, F32)
    for e in range(count):
        names = jnp.where(mine & (row == e), subset[e].astype(F32), names)
    share = keep.shape[0]
    for which, ref in ((half, keep), (1 - half, give)):
        for s in range(share):
            own = jnp.where(lax.div(spots[0], 2) == s, names, 0.0)
            ref[s, 0:coarse] = total[which * share + s].astype(BF16)
            rest = stack([mats[which * share + s], own], ref.shape[1] - coarse)
            ref[s, coarse:] = rest.astype(BF16)


def split(value):
    high = value.astype(BF16)
    return high, (value - high.astype(F32)).astype(BF16)


def coarse_body(own, other, subset, spots, y_all, near, far_y, names, held):
    groups, coarse, cols = y_all.shape
    share = groups // 2
    core = lax.rem(spots[0], 2)
    half = coarse // 2
    rights, blocks, thetas, ys = [], [], [], []
    for s in range(groups):
        both = (own[s] if s < share else other[s - share]).astype(F32)
        right = both[0:coarse]
        packed = both[coarse : coarse + half]
        block = jnp.concatenate([packed, pltpu.roll(packed, cols // 2, 1)], axis=0)
        theta = relax_coarse / jnp.maximum(packed[:, coarse : coarse + 1], 1.0)
        theta = jnp.concatenate([theta, theta], axis=0)
        high, low = split(block[:, 0:coarse])
        rights.append(right)
        blocks.append(jnp.concatenate([high, high, low], axis=1))
        thetas.append(theta)
        ys.append(theta * right)
    for sweep in range(CITER - 1):
        sides = []
        for s in range(groups):
            high, low = split(ys[s])
            sides.append(jnp.concatenate([high, low, high], axis=0))
        applied = [dot(blocks[s], sides[s]) for s in range(groups)]
        ys = [ys[s] + thetas[s] * (rights[s] - applied[s]) for s in range(groups)]
    for s in range(share):
        y_all[core * share + s] = ys[s].astype(BF16)
        y_all[(1 - core) * share + s] = ys[share + s].astype(BF16)
    for e in range(subset.shape[0]):
        held[e % 2, e // 2] = y_all[subset[e]]
    pack_sends(order(spots)[0], held[0], held[1], near, far_y)
    start = coarse + half
    count = names.shape[1]
    lane = lax.broadcasted_iota(jnp.int32, (count, cols), 1)
    for side in (0, 1):
        slot = lax.div(spots[1 + side], 2)
        far = own[slot].astype(F32)
        mine = (lane >= cols // 2) == (lax.rem(spots[1 + side], 2) == 1)
        far = jnp.where(mine, far[start : start + count], 0.0)
        names[side] = far + pltpu.roll(far, cols // 2, 1)


def second_body(resid, state, oper, outer, y_all, prolong, pf, names, face_source, subset, acc, second):
    coarse = y_all.shape[1]
    count, dof, _ = resid.shape
    inside, outside = [], []
    for e in range(count):
        i, j, k = place(e)
        step = dot(prolong[:, 0:coarse], y_all[subset[e]])
        second[e] = state[e] + step
        values = [step.astype(BF16)]
        for f, near, face in inner_faces(e):
            rows = dot(pf[face, :, 0:coarse], y_all[subset[near]]).astype(BF16)
            values.append(masked(face_source, e, f, rows))
        name = names[j, pl.ds(e ^ 2, 1), :]
        y_far = jnp.zeros(y_all.shape[1:], F32)
        for s in range(y_all.shape[0]):
            y_far = jnp.where(name == float(s), y_all[s].astype(F32), y_far)
        rows = dot(pf[3 - j, :, 0:coarse], y_far.astype(BF16)).astype(BF16)
        far = [jnp.zeros_like(rows), masked(face_source, e, 2 + j, rows)]
        inside.append(stack(values, 2 * dof))
        outside.append(stack(far, outer.shape[2]))
    for e in range(count):
        acc[e] = resid[e] - (dot(oper[e], inside[e]) + dot(outer[e], outside[e]))


def smooth_body(part, second, outer, inv, y1, y0, pf, face_source, spots, state, tr, s0, s1, s2, s3, tmp, sides, res):
    coarse = y0.shape[1]
    count = part.shape[0]
    rows = []
    for e in range(count):
        i = e % 2
        y_far = came(order(spots)[0], y0, y1, i, e // 2)
        value = dot(pf[1 - i, :, 0:coarse], y_far).astype(BF16)
        rows.append(stack([masked(face_source, e, i, value)], outer.shape[2]))
    for e in range(count):
        res[e] = (part[e] - dot(outer[e], rows[e])).astype(BF16)
    for e in range(count):
        state[e] = second[e] + relax_fine * dot(inv[e], res[e])
        emit_traces(e, state, tr, sides, tmp)
    emit_sends(spots, sides, (s0, s1, s2, s3))


def inner_body(rhs, state, oper, tr, face_source, acc):
    dof = state.shape[1]
    for e in range(state.shape[0]):
        values = [state[e].astype(BF16)] + [
            masked(face_source, e, f, tr[near, face]) for f, near, face in inner_faces(e)
        ]
        acc[e] = rhs[e].astype(F32) - dot(oper[e], stack(values, 2 * dof))


def final_body(part, state, outer, inv, xp, yp, xm, ym, face_source, spots, out_far, res, out, sems):
    count = state.shape[0]
    copies = chunks(count, ((out, out_far),), sems, OUT_PARTS)
    for e in range(count):
        far = stack(pick(e, (xm, xp, ym, yp), face_source, spots), outer.shape[2])
        res[e] = (part[e] - dot(outer[e], far)).astype(BF16)
    size = count // OUT_PARTS
    for e in range(count):
        out[e] = state[e] + relax_fine * dot(inv[e], res[e])
        if e % size == size - 1:
            copies[e // size][0].start()
    for (copy,) in copies:
        copy.wait()


def swap(value, axis, start):
    count = lax.axis_size(axis)
    pairs = [(i % count, (i + 1) % count) for i in range(start, count, 2)]
    return lax.ppermute(value, axis, pairs + [(b, a) for a, b in pairs])


def exchange(sends):
    x0, x1, y0, y1 = sends
    x1 = swap(x1, "gx", 1)
    y1 = swap(y1, "gy", 1)
    x0 = swap(x0, "gx", 0)
    y0 = swap(y0, "gy", 0)
    return x0, x1, y0, y1


def plus(one, two):
    return (one.astype(F32) + two.astype(F32)).astype(BF16)


def row_sum(keep, give):
    count = lax.axis_size("gy")
    part = plus(keep, swap(give, "gy", 0))
    pairs = not count & (count - 1)
    parts = [part] + [
        lax.ppermute(part, "gy", [(i, i ^ step if pairs else (i + step) % count) for i in range(count)])
        for step in range(2, count, 2)
    ]
    return sum(part.astype(F32) for part in parts).astype(BF16)


def on_device(rhs, diag_blocks, inverse_blocks, couplings, prolong, face_source, subset):
    elements, dof, cols = rhs.shape
    fdof = couplings.shape[3]
    coarse = prolong.shape[1]
    groups = lax.axis_size("gy")
    half = elements // 2
    shape = jax.ShapeDtypeStruct
    state_s = shape((elements, dof, cols), F32)
    tr_s = shape((elements, 6, fdof, cols), BF16)
    sends_s = [shape((half, fdof, cols), BF16)] * 4
    y_s = shape((half, coarse, cols), BF16)
    near_rows = -(-2 * fdof // cols) * cols
    message = -(-(coarse + coarse // 2 + elements) // 16) * 16
    tmps = pltpu.VMEM((elements, 2, fdof, cols), F32)
    sides = pltpu.VMEM((4, half, fdof, cols), BF16)
    state_b = pltpu.VMEM((elements, dof, cols), BF16)
    apply_flops = 2 * elements * dof * cols * (dof + 3 * fdof)
    inv_flops = 2 * elements * dof * dof * cols
    far_flops = 4 * elements * dof * fdof * cols
    coup = jnp.swapaxes(couplings, 2, 3)
    pt = prolong.T

    me = lax.axis_index("gy")
    spots = jnp.stack(
        [me, (me + groups - 1) % groups, (me + 1) % groups, lax.axis_index("gx")]
    ).astype(jnp.int32)
    first, tr, rhs, inv, coup, *sends = run(
        first_body,
        (rhs, inverse_blocks, coup, spots),
        [state_s, tr_s] + [shape(a.shape, BF16) for a in (rhs, inverse_blocks, coup)] + sends_s,
        [tmps, sides, pltpu.SemaphoreType.DMA((2, PARTS + 1))],
        inv_flops,
        far_ins=(0, 1, 2),
    )
    xm, xp, ym, yp = exchange(sends)
    acc, mats, oper, outer, pf, wide = run(
        local_body,
        (rhs, first, diag_blocks, coup, tr, pt, face_source, subset),
        [
            state_s,
            shape((groups, coarse // 2, cols), F32),
            shape((elements, dof, 2 * dof), BF16),
            shape((elements, dof, near_rows), BF16),
            shape((6, fdof, cols), BF16),
            shape((dof, cols), BF16),
        ],
        [
            pltpu.VMEM((dof, cols), F32),
            pltpu.VMEM((2, fdof, cols), F32),
            pltpu.VMEM((groups, coarse, cols), F32),
        ],
        2 * apply_flops,
    )
    resid, keep, give = run(
        restrict_body,
        (acc, outer, xp, yp, xm, ym, pt, mats, face_source, subset, spots),
        [state_s] + [shape((groups // 2, message, cols), BF16)] * 2,
        [pltpu.VMEM((groups, coarse, cols), F32)],
        far_flops,
    )
    own = row_sum(keep, give)
    y_all, y0, y1, names = run(
        coarse_body,
        (own, swap(own, "gy", 0), subset, spots),
        [shape((groups, coarse, cols), BF16), y_s, y_s, shape((2, elements, cols), F32)],
        [pltpu.VMEM((2, half, coarse, cols), BF16)],
        6 * groups * coarse * coarse * cols * CITER,
    )
    y1 = swap(y1, "gx", 1)
    y0 = swap(y0, "gx", 0)
    acc, second = run(
        second_body,
        (resid, first, oper, outer, y_all, wide, pf, names, face_source, subset),
        [state_s, state_s],
        [],
        apply_flops,
    )
    state, tr, *sends = run(
        smooth_body,
        (acc, second, outer, inv, y1, y0, pf, face_source, spots),
        [state_s, tr_s] + sends_s,
        [tmps, sides, state_b],
        inv_flops,
    )
    xm, xp, ym, yp = exchange(sends)
    acc = run(inner_body, (rhs, state, oper, tr, face_source), [state_s], [], apply_flops)[0]
    return run(
        final_body,
        (acc, state, outer, inv, xp, yp, xm, ym, face_source, spots),
        [state_s],
        [state_b, pltpu.VMEM((elements, dof, cols), F32), pltpu.SemaphoreType.DMA((1, elements))],
        inv_flops + far_flops,
        far_outs=(0,),
    )[0]


def solution(mesh):
    return jax.shard_map(
        on_device,
        mesh=mesh,
        in_specs=(
            P(("gx", "gy"), None, None),
            P(("gx", "gy"), None, None),
            P(("gx", "gy"), None, None),
            P(("gx", "gy"), None, None, None),
            P(),
            P(("gx", "gy"), None),
            P(("gx", "gy")),
        ),
        out_specs=P(("gx", "gy"), None, None),
        check_vma=False,
    )
```
